32 devices in a mesh: pb: 2 (over x), ka: 4 (over z), ha: 4 (over y, core).
Axes of the slice: x: 2, y: 2, z: 4, core: 2. Of those that a mesh axis runs over, the one named last changes fastest.
Arguments:
- queries: bfloat16 [768, 64, 128], P('pb', 'ha'), may hold values from -6 to 6
- key_codes: bfloat16 [768, 8, 128], P('ka', 'ha'), may hold values from -4 to 4
- key_scale_powers: int32 [12, 8], P('ka', 'ha'), may hold values from -1 to 1
- values: bfloat16 [768, 8, 128], P('ka', 'ha'), may hold values from -6 to 6
- grad_out: bfloat16 [768, 64, 128], P('pb', 'ha'), may hold values from -1.5 to 1.5
- grad_dot: float32 [768, 64], P('pb', 'ha'), may hold values from -6 to 6
- log_totals: float32 [768, 64], P('pb', 'ha')
Outputs:
- grad_queries: bfloat16 [768, 64, 128], P(('pb', 'ka'), 'ha')
- grad_keys: bfloat16 [768, 8, 128], P('ka', 'ha')
- grad_values: bfloat16 [768, 8, 128], P('ka', 'ha')
The draws below stay inside these ranges and needn't reach their ends.
All inputs are finite; a program needn't handle non-finite values.
Results may differ from the reference program's by a relative error of at most 0.012.
Values may be sent and summed in bfloat16 or wider, within the bound.
No kernel may reach another device: no remote copies, remote signals or barrier semaphores. Data moves between devices by JAX's collectives and lax.ppermute only.
A program may use at most 64 MiB of HBM per device.

```python
import jax
import jax.numpy as jnp
from jax import lax

KEY_VALUE_HEADS = 8
HEAD_SIZE = 128
KEYS_PER_SCALE = 64
QUERY_HEADS = 64
WINDOW_TOKENS = 768


def draw_key_codes(key, part):
    first_part, second_part = jax.random.split(jax.random.fold_in(key, 11))
    start_offsets = jax.random.uniform(first_part, (1, KEY_VALUE_HEADS, HEAD_SIZE), jnp.float32, -0.4, 0.4)
    fraction = jnp.arange(WINDOW_TOKENS, dtype=jnp.float32)[:, None, None] / (WINDOW_TOKENS - 1)
    ramp = 1.0 + 2.0 * fraction
    random_jitter = 0.6 * jax.random.normal(second_part, (WINDOW_TOKENS, KEY_VALUE_HEADS, HEAD_SIZE), jnp.float32)
    return jnp.clip(start_offsets * ramp + random_jitter, -4.0, 4.0).astype(jnp.bfloat16)


def draw_log_totals(key, part):
    inner = jax.random.fold_in(key, 23)
    level = jnp.log(1.0 + WINDOW_TOKENS * jnp.ones((WINDOW_TOKENS, 1), jnp.float32))
    extra = jax.random.uniform(inner, (WINDOW_TOKENS, QUERY_HEADS), jnp.float32, 0.5, 1.5)
    return level + extra


def touch_ends(entries, rng, low, top_value):
    spot = [jax.random.randint(jax.random.fold_in(rng, axis), (), 0, length) for axis, length in enumerate(entries.shape)]
    longest = entries.shape.index(max(entries.shape))
    neighbour = spot[:longest] + [(spot[longest] + 1) % entries.shape[longest]] + spot[longest + 1:]
    return entries.at[tuple(spot)].set(low).at[tuple(neighbour)].set(top_value)


def block_levels(own_key, shape, shards, smallest, high):
    factor_of, own = 1.0, jax.random.fold_in(own_key, 6)
    for axis_at, parts in shards:
        steps = jnp.exp(jax.random.uniform(jax.random.fold_in(own, axis_at), (parts,), jnp.float32, smallest / len(shards), high / len(shards)))
        factor_of = factor_of * jnp.repeat(steps, shape[axis_at] // parts).reshape([-1 if axis == axis_at else 1 for axis in range(len(shape))])
    return factor_of


def gaussian(key, extent, scale, most, pieces=(), kind=jnp.bfloat16):
    entries = scale * jax.random.normal(key, extent, jnp.float32)
    if pieces:
        entries = entries * block_levels(key, extent, pieces, -0.22, 0.18)
    return jnp.clip(entries, -most, most).astype(kind)


def setup_inputs(seed: int = 0) -> dict:
    arg_keys = jax.random.split(jax.random.key(seed), 8)
    queries = gaussian(arg_keys[0], (WINDOW_TOKENS, QUERY_HEADS, HEAD_SIZE), 1.0, 6.0, ((0, 2), (1, 4)))
    key_codes = draw_key_codes(jax.random.fold_in(arg_keys[7], 71), 0)
    key_scale_powers = touch_ends(jax.random.randint(arg_keys[2], (WINDOW_TOKENS // KEYS_PER_SCALE, KEY_VALUE_HEADS), -1, 2), jax.random.fold_in(arg_keys[2], 1), -1, 1).astype(jnp.int32)
    values = gaussian(arg_keys[3], (WINDOW_TOKENS, KEY_VALUE_HEADS, HEAD_SIZE), 1.0, 6.0, ((0, 4), (1, 4)))
    grad_out = gaussian(arg_keys[4], (WINDOW_TOKENS, QUERY_HEADS, HEAD_SIZE), 0.25, 1.5, ((0, 2), (1, 4)))
    grad_dot = gaussian(arg_keys[5], (WINDOW_TOKENS, QUERY_HEADS), 1.0, 6.0, ((0, 2), (1, 4)), jnp.float32)
    log_totals = draw_log_totals(jax.random.fold_in(arg_keys[7], 71), 0)
    return dict(queries=queries, key_codes=key_codes, key_scale_powers=key_scale_powers, values=values, grad_out=grad_out, grad_dot=grad_dot, log_totals=log_totals)


def grads_one(item):
    query_block, grad_block, dot_block, total_block, key_block, value_block = item
    inverse_root = HEAD_SIZE ** -0.5
    positions = jnp.arange(WINDOW_TOKENS, dtype=jnp.int32)
    visible = positions[None, :] <= positions[:, None]
    query_wide = query_block.astype(jnp.float32)
    grad_wide = grad_block.astype(jnp.float32)
    key_wide = key_block.astype(jnp.float32)
    value_wide = value_block.astype(jnp.float32)
    scores = jnp.einsum("igd,jd->gij", query_wide, key_wide) * inverse_root
    weights = jnp.where(visible[None], jnp.exp(scores - total_block.T[:, :, None]), 0.0)
    weights_low = weights.astype(jnp.bfloat16).astype(jnp.float32)
    grad_values = jnp.einsum("gij,igd->jd", weights_low, grad_wide)
    grad_weights = jnp.einsum("igd,jd->gij", grad_wide, value_wide)
    grad_scores = (weights * (grad_weights - dot_block.T[:, :, None])).astype(jnp.bfloat16).astype(jnp.float32)
    grad_query = jnp.einsum("gij,jd->igd", grad_scores, key_wide) * inverse_root
    grad_keys = jnp.einsum("gij,igd->jd", grad_scores, query_wide) * inverse_root
    return grad_query.astype(jnp.bfloat16), grad_keys.astype(jnp.bfloat16), grad_values.astype(jnp.bfloat16)


def reference(queries, key_codes, key_scale_powers, values, grad_out, grad_dot, log_totals):
    queries_per_group = QUERY_HEADS // KEY_VALUE_HEADS
    factor = jnp.exp2(key_scale_powers.astype(jnp.float32))
    dequantized = key_codes.astype(jnp.float32) * jnp.repeat(factor, KEYS_PER_SCALE, axis=0)[:, :, None]
    key_means = jnp.sum(dequantized, axis=0) / WINDOW_TOKENS
    smoothed = (dequantized - key_means).astype(jnp.bfloat16)

    def by_group(input_matrix):
        return jnp.swapaxes(input_matrix.reshape((WINDOW_TOKENS, KEY_VALUE_HEADS, queries_per_group) + input_matrix.shape[2:]), 0, 1)

    items = (by_group(queries), by_group(grad_out), by_group(grad_dot), by_group(log_totals),
             jnp.swapaxes(smoothed, 0, 1), jnp.swapaxes(values, 0, 1))
    grad_query, grad_keys, grad_values = lax.map(grads_one, items)
    grad_query = jnp.swapaxes(grad_query, 0, 1).reshape(WINDOW_TOKENS, QUERY_HEADS, HEAD_SIZE)
    return grad_query, jnp.swapaxes(grad_keys, 0, 1), jnp.swapaxes(grad_values, 0, 1)
```

```python
import functools
import math

import jax
import jax.numpy as jnp
from jax import lax
from jax.experimental import pallas as pl
from jax.experimental.pallas import tpu as pltpu
from jax.sharding import PartitionSpec as P

KEYS_PER_SCALE = 64
LOG2E = math.log2(math.e)
VMEM = pl.BlockSpec(memory_space=pltpu.VMEM)
SMEM = pl.BlockSpec(memory_space=pltpu.SMEM)
NT = (((1,), (1,)), ((), ()))
SUM_ROWS = 8


def prep_kernel(powers_ref, codes_ref, values_ref, packed_ref, sums_ref):
    key_count, kv_heads, width = codes_ref.shape
    rows = lax.broadcasted_iota(jnp.int32, (key_count, width), 0) // KEYS_PER_SCALE
    sums_ref[...] = jnp.zeros_like(sums_ref)
    codes = codes_ref[...].astype(jnp.float32)
    values = values_ref[...].astype(jnp.float32)
    for g in range(kv_heads):
        factor = jnp.zeros((key_count, width), jnp.float32)
        for b in range(key_count // KEYS_PER_SCALE):
            power = jnp.left_shift(1, powers_ref[b, g] + 8).astype(jnp.float32) * 2.0**-8
            factor = jnp.where(rows == b, power, factor)
        wide = codes[:, g, :] * factor
        packed_ref[g] = wide.astype(jnp.bfloat16)
        packed_ref[kv_heads + g] = values[:, g, :].astype(jnp.bfloat16)
        sums_ref[pl.ds(g, 1)] = jnp.sum(wide, axis=0, keepdims=True)


def rows_kernel(
    shifts, share, kv_heads, key_devices, first,
    q_ref, do_ref, stats_ref, own_ref, got_ref, *refs,
):
    if first:
        sums_ref, dq_ref, acc_ref, smooth_ref = refs
    else:
        smooth_ref, acc_in_ref, dq_ref, keep_ref, send_ref = refs
    ka, pb = lax.axis_index("ka"), lax.axis_index("pb")
    key_count, width = own_ref.shape[1:]
    heads = q_ref.shape[1]
    group = heads // kv_heads
    cols = share * group
    root = width**-0.5
    own_base, got_base = ka * key_count, (ka ^ 1) * key_count
    line = lax.broadcasted_iota(jnp.int32, (2 * key_count, cols), 0)
    key_pos = line + jnp.where(line < key_count, own_base, got_base - key_count)
    lead = key_pos - lax.broadcasted_iota(jnp.int32, (2 * key_count, cols), 1) // group
    smooth, turned, vals = [], [], []
    for g in range(kv_heads):
        if first:
            own = own_ref[g].astype(jnp.float32)
            got = got_ref[g].astype(jnp.float32)
            total = jnp.sum(own, axis=0, keepdims=True) + jnp.sum(got, axis=0, keepdims=True)
            total = total + sums_ref[pl.ds(g, 1)]
            mean = total / (key_count * key_devices)
            k = jnp.concatenate([own - mean, got - mean], axis=0).astype(jnp.bfloat16)
            smooth_ref[g] = k
        else:
            k = smooth_ref[g]
        smooth.append(k)
        turned.append(k.astype(jnp.float32).T.astype(jnp.bfloat16))
        vals.append(jnp.concatenate([own_ref[kv_heads + g], got_ref[kv_heads + g]], axis=0))
    dks = [None] * kv_heads
    dvs = [None] * kv_heads
    for at, shift in enumerate(shifts):
        block = lax.rem(ka + shift, key_devices)
        q_all = q_ref[pl.ds(block * share, share)].astype(jnp.float32)
        do_all = do_ref[pl.ds(block * share, share)].astype(jnp.float32)
        visible = lead <= pb * (share * key_devices) + block * share
        outs = []
        for g in range(kv_heads):
            chosen = slice(g * group, (g + 1) * group)
            q = q_all[:, chosen].reshape(cols, width).astype(jnp.bfloat16)
            do = do_all[:, chosen].reshape(cols, width).astype(jnp.bfloat16)
            log_total = stats_ref[block, pl.ds(g, 1), :]
            dot = stats_ref[block, pl.ds(kv_heads + g, 1), :]
            scores = lax.dot_general(smooth[g], q, NT, preferred_element_type=jnp.float32)
            weights = jnp.where(visible, jnp.exp2(scores * (root * LOG2E) - log_total), 0.0)
            dp = lax.dot_general(vals[g], do, NT, preferred_element_type=jnp.float32)
            ds = (weights * (dp - dot)).astype(jnp.bfloat16)
            dv = jnp.dot(weights.astype(jnp.bfloat16), do, preferred_element_type=jnp.float32)
            dk = jnp.dot(ds, q, preferred_element_type=jnp.float32)
            dvs[g] = dv if dvs[g] is None else dvs[g] + dv
            dks[g] = dk if dks[g] is None else dks[g] + dk
            dq = jnp.dot(turned[g], ds, preferred_element_type=jnp.float32).T * root
            outs.append(dq.reshape(share, group, width))
        dq_ref[at] = jnp.concatenate(outs, axis=1).astype(dq_ref.dtype)
    for g in range(kv_heads):
        if first:
            acc_ref[g] = dks[g]
            acc_ref[kv_heads + g] = dvs[g]
        else:
            dk = (acc_in_ref[g] + dks[g]) * root
            dv = acc_in_ref[kv_heads + g] + dvs[g]
            for j, whole in ((g, dk), (kv_heads + g, dv)):
                keep_ref[j] = whole[:key_count]
                send_ref[j] = whole[key_count:].astype(jnp.bfloat16)


def finish_kernel(mine_ref, other_ref, dk_ref, dv_ref):
    kv_heads = mine_ref.shape[0] // 2
    total = mine_ref[...].astype(jnp.float32) + other_ref[...].astype(jnp.float32)
    for ref, base in ((dk_ref, 0), (dv_ref, kv_heads)):
        for g in range(kv_heads):
            ref[:, g, :] = total[base + g]


def cost(flops, size):
    return pl.CostEstimate(flops=int(flops), bytes_accessed=int(size), transcendentals=0)


def per_device(queries, key_codes, key_scale_powers, values, grad_out, grad_dot, log_totals):
    query_count, head_count, width = queries.shape
    key_count, kv_heads, _ = key_codes.shape
    group = head_count // kv_heads
    key_devices = lax.axis_size("ka")
    query_devices = lax.axis_size("pb")
    share = query_count // key_devices
    params = pltpu.CompilerParams(vmem_limit_bytes=40 * 2**20)

    def turn(x, by):
        return lax.ppermute(x, "ka", [((i + by) % key_devices, i) for i in range(key_devices)])

    def swap(x, by):
        return lax.ppermute(x, "ka", [(i, i ^ by) for i in range(key_devices)])

    packed, sums = pl.pallas_call(
        prep_kernel,
        out_shape=(
            jax.ShapeDtypeStruct((2 * kv_heads, key_count, width), jnp.bfloat16),
            jax.ShapeDtypeStruct((SUM_ROWS, width), jnp.float32),
        ),
        in_specs=[SMEM, VMEM, VMEM],
        out_specs=(VMEM, VMEM),
        compiler_params=params,
        name="prep",
    )(key_scale_powers, key_codes, values)
    got = swap(packed, 1)
    others = sum(swap(sums, by) for by in range(2, key_devices))

    def by_head(x):
        x = x.reshape(key_devices, share, kv_heads, group)
        return x.transpose(0, 2, 1, 3).reshape(key_devices, kv_heads, share * group)

    stats = jnp.concatenate([by_head(log_totals * LOG2E), by_head(grad_dot)], axis=1)

    even = list(range(2, key_devices, 2))
    acc_shape = jax.ShapeDtypeStruct((2 * kv_heads, 2 * key_count, width), jnp.float32)
    smooth_shape = jax.ShapeDtypeStruct((kv_heads, 2 * key_count, width), jnp.bfloat16)
    half = 10 * key_count * 2 * width * share * head_count

    sent, acc, smooth = pl.pallas_call(
        functools.partial(rows_kernel, even, share, kv_heads, key_devices, True),
        out_shape=(
            jax.ShapeDtypeStruct((len(even), share, head_count, width), jnp.bfloat16),
            acc_shape,
            smooth_shape,
        ),
        in_specs=[VMEM] * 6,
        out_specs=(VMEM,) * 3,
        compiler_params=params,
        cost_estimate=cost(half * len(even), 4 * 2**20),
        name="cross_rows",
    )(queries, grad_out, stats, packed, got, others)
    back = [turn(sent[at], key_devices - by) for at, by in enumerate(even)]

    own_dq, keep, send = pl.pallas_call(
        functools.partial(rows_kernel, [0], share, kv_heads, key_devices, False),
        out_shape=(
            jax.ShapeDtypeStruct((1, share, head_count, width), jnp.float32),
            jax.ShapeDtypeStruct((2 * kv_heads, key_count, width), jnp.float32),
            jax.ShapeDtypeStruct((2 * kv_heads, key_count, width), jnp.bfloat16),
        ),
        in_specs=[VMEM] * 7,
        out_specs=(VMEM,) * 3,
        compiler_params=params,
        cost_estimate=cost(half, 4 * 2**20),
        name="own_rows",
    )(queries, grad_out, stats, packed, got, smooth, acc)
    mine = (keep + swap(send, 1).astype(jnp.float32)).astype(jnp.bfloat16)
    if query_devices == 2:
        other = lax.ppermute(mine, "pb", [(0, 1), (1, 0)])
    else:
        other = lax.psum(mine.astype(jnp.float32), "pb") - mine.astype(jnp.float32)
    total = mine.astype(jnp.float32) + other.astype(jnp.float32)
    total = total.reshape(2, kv_heads, key_count, width).swapaxes(1, 2).astype(jnp.bfloat16)
    query_out = own_dq[0]
    for piece in back:
        query_out = query_out + piece.astype(jnp.float32)
    return query_out.astype(jnp.bfloat16), total[0], total[1]


def solution(mesh):
    in_specs = (
        P("pb", "ha", None),
        P("ka", "ha", None),
        P("ka", "ha"),
        P("ka", "ha", None),
        P("pb", "ha", None),
        P("pb", "ha"),
        P("pb", "ha"),
    )
    out_specs = (P(("pb", "ka"), "ha", None), P("ka", "ha", None), P("ka", "ha", None))
    return jax.shard_map(
        per_device, mesh=mesh, in_specs=in_specs, out_specs=out_specs, check_vma=False
    )
```

```python
import functools
import math

import jax
import jax.numpy as jnp
from jax import lax
from jax.experimental import pallas as pl
from jax.experimental.pallas import tpu as pltpu
from jax.sharding import PartitionSpec as P

KEYS_PER_SCALE = 64
LOG2E = math.log2(math.e)
VMEM = pl.BlockSpec(memory_space=pltpu.VMEM)
SMEM = pl.BlockSpec(memory_space=pltpu.SMEM)
HBM = pl.BlockSpec(memory_space=pltpu.HBM)
NT = (((1,), (1,)), ((), ()))
SUM_ROWS = 16


def prep_kernel(powers_ref, codes_hbm, values_hbm, *refs):
    *message_refs, sums_ref, codes_ref, values_ref, sems = refs
    key_count, kv_heads, width = codes_ref.shape
    load_codes = pltpu.make_async_copy(codes_hbm, codes_ref, sems.at[0])
    load_values = pltpu.make_async_copy(values_hbm, values_ref, sems.at[1])
    load_codes.start()
    load_values.start()
    rows = lax.broadcasted_iota(jnp.int32, (key_count, width), 0) // KEYS_PER_SCALE
    factors = []
    for g in range(kv_heads):
        factor = jnp.zeros((key_count, width), jnp.float32)
        for b in range(key_count // KEYS_PER_SCALE):
            power = jnp.left_shift(1, powers_ref[g, b] + 8).astype(jnp.float32) * 2.0**-8
            factor = jnp.where(rows == b, power, factor)
        factors.append(factor)
    load_codes.wait()
    load_values.wait()
    codes = codes_ref[...].astype(jnp.float32)
    values = values_ref[...].astype(jnp.float32)
    sums = []
    for g in range(kv_heads):
        wide = codes[:, g, :] * factors[g]
        message_refs[g][0:key_count] = wide.astype(jnp.bfloat16)
        message_refs[g][key_count : 2 * key_count] = values[:, g, :].astype(jnp.bfloat16)
        sums.append(jnp.sum(wide, axis=0, keepdims=True))
    line = lax.broadcasted_iota(jnp.int32, (SUM_ROWS, width), 0)
    parts = jnp.zeros((SUM_ROWS, width), jnp.float32)
    whole = jnp.zeros((SUM_ROWS, width), jnp.float32)
    for g in range(kv_heads):
        rest = sums[g]
        whole = jnp.where(line == g, rest, whole)
        for j in range(3):
            piece = rest.astype(jnp.bfloat16).astype(jnp.float32)
            parts = jnp.where(line == 3 * g + j, piece, parts)
            rest = rest - piece
    sums_ref[...] = whole
    for ref in message_refs:
        ref[2 * key_count : 2 * key_count + SUM_ROWS] = parts.astype(jnp.bfloat16)


def gather_kernel(row_sets, share, q_hbm, do_hbm, q_out, do_out, q_ref, do_ref, sems):
    ka = lax.axis_index("ka")
    kv_heads = len(row_sets)
    group = q_ref.shape[2] // kv_heads
    cols, width = share * group, q_ref.shape[3]
    needed = sorted({m for sets in row_sets for m in sets})
    loads = []
    for at, m in enumerate(needed):
        for j, (src, dst) in enumerate(((q_hbm, q_ref), (do_hbm, do_ref))):
            load = pltpu.make_async_copy(
                src.at[pl.ds((ka ^ m) * share, share)], dst.at[at], sems.at[2 * at + j]
            )
            load.start()
            loads.append(load)
    for at, m in enumerate(needed):
        for j, (src, dst) in enumerate(((q_ref, q_out), (do_ref, do_out))):
            loads[2 * at + j].wait()
            wide = src[at].astype(jnp.float32)
            for g in range(kv_heads):
                if m in row_sets[g]:
                    rows = wide[:, g * group : (g + 1) * group].reshape(cols, width)
                    dst[g, row_sets[g].index(m)] = rows.astype(jnp.bfloat16)


def rows_kernel(key_devices, share, partners, row_sets, *refs):
    kv_heads = len(partners)
    q_ref, do_ref, stats_ref = refs[:3]
    own_refs, got_refs = refs[3 : 3 + kv_heads], refs[3 + kv_heads : 3 + 2 * kv_heads]
    dq_ref, cross_ref, keep_ref = refs[-3:]
    send_refs = refs[-3 - kv_heads : -3]
    sum_refs = refs[3 + 2 * kv_heads : -3 - kv_heads]
    ka, pb = lax.axis_index("ka"), lax.axis_index("pb")
    cols, width = q_ref.shape[2:]
    key_count = (own_refs[0].shape[0] - SUM_ROWS) // 2
    group = cols // share
    root = width**-0.5
    line = lax.broadcasted_iota(jnp.int32, (2 * key_count, cols), 0)
    step = lax.broadcasted_iota(jnp.int32, (2 * key_count, cols), 1) // group
    parts = own_refs[0][2 * key_count :].astype(jnp.float32)
    for partner in dict(zip(partners, range(kv_heads))).values():
        parts = parts + got_refs[partner][2 * key_count :].astype(jnp.float32)
    whole = jnp.zeros((SUM_ROWS, width), jnp.float32)
    for ref in sum_refs:
        whole = whole + ref[...]
    for g in range(kv_heads):
        own, got = own_refs[g], got_refs[g]
        total = jnp.sum(parts[3 * g : 3 * g + 3], axis=0, keepdims=True) + whole[g : g + 1]
        mean = total / (key_count * key_devices)
        k = jnp.concatenate([own[0:key_count], got[0:key_count]], axis=0).astype(jnp.float32)
        k = k - mean
        turned = k.T.astype(jnp.bfloat16)
        k = k.astype(jnp.bfloat16)
        v = jnp.concatenate(
            [own[key_count : 2 * key_count], got[key_count : 2 * key_count]], axis=0
        )
        base = jnp.where(line < key_count, ka * key_count, ((ka ^ partners[g]) - 1) * key_count)
        lead = line + base - step
        dk = dv = None
        for at, m in enumerate(row_sets[g]):
            block = ka ^ m
            q, do = q_ref[g, at], do_ref[g, at]
            log_total = stats_ref[block, pl.ds(g, 1), :]
            dot = stats_ref[block, pl.ds(kv_heads + g, 1), :]
            visible = lead <= pb * (share * key_devices) + block * share
            scores = lax.dot_general(k, q, NT, preferred_element_type=jnp.float32)
            weights = jnp.where(visible, jnp.exp2(scores * (root * LOG2E) - log_total), 0.0)
            dp = lax.dot_general(v, do, NT, preferred_element_type=jnp.float32)
            ds = (weights * (dp - dot)).astype(jnp.bfloat16)
            dv_now = jnp.dot(weights.astype(jnp.bfloat16), do, preferred_element_type=jnp.float32)
            dk_now = jnp.dot(ds, q, preferred_element_type=jnp.float32)
            dv = dv_now if dv is None else dv + dv_now
            dk = dk_now if dk is None else dk + dk_now
            dq = jnp.dot(turned, ds, preferred_element_type=jnp.float32).T * root
            if m == 0:
                dq_ref[g] = dq
            else:
                others = [other for other in row_sets[g] if other]
                send_refs[g][others.index(m)] = dq.astype(jnp.bfloat16)
        for j, grad in ((2 * g, dk * root), (2 * g + 1, dv)):
            keep_ref[j] = grad[:key_count].astype(jnp.bfloat16)
            cross_ref[j] = grad[key_count:].astype(jnp.bfloat16)


def across_kernel(*refs):
    *in_refs, out_a, out_b = refs
    total = in_refs[0][...].astype(jnp.float32)
    for ref in in_refs[1:]:
        total = total + ref[...].astype(jnp.float32)
    half = out_a.shape[0]
    out_a[...] = total[:half].astype(jnp.bfloat16)
    out_b[...] = total[half:].astype(jnp.bfloat16)


def finish_kernel(kv_heads, keep_count, own_dq_ref, *refs):
    *refs, dq_ref, dk_ref, dv_ref = refs
    keep_refs, refs = refs[:keep_count], refs[keep_count:]
    z_refs, back_refs = refs[:2], refs[2:]
    share, heads, width = dq_ref.shape
    group = heads // kv_heads
    outs = []
    for g in range(kv_heads):
        dq = own_dq_ref[g]
        for ref in back_refs[g :: kv_heads]:
            dq = dq + ref[...].astype(jnp.float32)
        outs.append(dq.reshape(share, group, width))
    dq_ref[...] = jnp.concatenate(outs, axis=1).astype(jnp.bfloat16)
    total = keep_refs[0][...].astype(jnp.float32)
    for ref in keep_refs[1:]:
        total = total + ref[...].astype(jnp.float32)
    total = total + jnp.concatenate([ref[...] for ref in z_refs], axis=0).astype(jnp.float32)
    for j, ref in enumerate((dk_ref, dv_ref)):
        grads = jnp.stack([total[2 * g + j] for g in range(kv_heads)], axis=1)
        ref[...] = grads.astype(jnp.bfloat16)


def per_device(queries, key_codes, key_scale_powers, values, grad_out, grad_dot, log_totals):
    query_count, head_count, width = queries.shape
    key_count, kv_heads, _ = key_codes.shape
    group = head_count // kv_heads
    key_devices = lax.axis_size("ka")
    query_devices = lax.axis_size("pb")
    share = query_count // key_devices
    cols = share * group
    params = pltpu.CompilerParams(vmem_limit_bytes=24 * 2**20)
    top = key_devices // 2
    partners = [1 if g < kv_heads // 2 else top for g in range(kv_heads)]
    row_sets = [[m for m in range(key_devices) if not m & p] for p in partners]
    shape = jax.ShapeDtypeStruct

    def swap(x, by):
        return lax.ppermute(x, "ka", [(i, i ^ by) for i in range(key_devices)])

    def pinned(x):
        return pltpu.with_memory_space_constraint(x, pltpu.HBM)

    *messages, sums = pl.pallas_call(
        prep_kernel,
        out_shape=(shape((2 * key_count + SUM_ROWS, width), jnp.bfloat16),) * kv_heads
        + (shape((SUM_ROWS, width), jnp.float32),),
        in_specs=[SMEM, HBM, HBM],
        out_specs=(VMEM,) * (kv_heads + 1),
        scratch_shapes=[
            pltpu.VMEM(key_codes.shape, key_codes.dtype),
            pltpu.VMEM(values.shape, values.dtype),
            pltpu.SemaphoreType.DMA((2,)),
        ],
        compiler_params=params,
        name="prep",
    )(key_scale_powers.T, pinned(key_codes), pinned(values))
    got = [swap(message, by) for message, by in zip(messages, partners)]
    others = [swap(sums, by) for by in range(1, key_devices) if by not in partners]

    needed = sorted({m for sets in row_sets for m in sets})
    laid = shape((kv_heads, key_devices // 2, cols, width), jnp.bfloat16)
    rows_q, rows_do = pl.pallas_call(
        functools.partial(gather_kernel, row_sets, share),
        out_shape=(laid, laid),
        in_specs=[HBM, HBM],
        out_specs=(VMEM, VMEM),
        scratch_shapes=[
            pltpu.VMEM((len(needed), share, head_count, width), queries.dtype),
            pltpu.VMEM((len(needed), share, head_count, width), grad_out.dtype),
            pltpu.SemaphoreType.DMA((2 * len(needed),)),
        ],
        compiler_params=params,
        name="gather",
    )(pinned(queries), pinned(grad_out))

    stats = jnp.concatenate([log_totals.T * LOG2E, grad_dot.T], axis=0)
    stats = stats.reshape(2 * kv_heads, group, key_devices, share)
    stats = stats.transpose(2, 0, 3, 1).reshape(key_devices, 2 * kv_heads, cols)

    part = shape((2 * kv_heads, key_count, width), jnp.bfloat16)
    sent = shape((key_devices // 2 - 1, cols, width), jnp.bfloat16)
    *sends, own_dq, cross, keep = pl.pallas_call(
        functools.partial(rows_kernel, key_devices, share, partners, row_sets),
        out_shape=(sent,) * kv_heads + (shape((kv_heads, cols, width), jnp.float32), part, part),
        in_specs=[VMEM] * (3 + 2 * kv_heads + len(others)),
        out_specs=(VMEM,) * (kv_heads + 3),
        compiler_params=params,
        name="rows",
    )(rows_q, rows_do, stats, *messages, *got, *others)

    def over_queries(x):
        if query_devices == 2:
            return [x, lax.ppermute(x, "pb", [(0, 1), (1, 0)])]
        return [lax.psum(x.astype(jnp.float32), "pb")]

    crossed = over_queries(cross)
    back = []
    for at in range(key_devices // 2 - 1):
        for g in range(kv_heads):
            back.append(swap(sends[g][at], [m for m in row_sets[g] if m][at]))
    kept = over_queries(keep)
    half = shape((kv_heads, key_count, width), jnp.bfloat16)
    z_a, z_b = pl.pallas_call(
        across_kernel,
        out_shape=(half, half),
        in_specs=[VMEM] * len(crossed),
        out_specs=(VMEM, VMEM),
        compiler_params=params,
        cost_estimate=pl.CostEstimate(
            flops=10**10, bytes_accessed=2**20, transcendentals=0
        ),
        name="across",
    )(*crossed)
    z = [swap(z_a, partners[0]), swap(z_b, partners[-1])]
    return pl.pallas_call(
        functools.partial(finish_kernel, kv_heads, len(kept)),
        out_shape=(
            shape((share, head_count, width), jnp.bfloat16),
            shape(key_codes.shape, jnp.bfloat16),
            shape(values.shape, jnp.bfloat16),
        ),
        in_specs=[VMEM] * (1 + len(kept) + len(z) + len(back)),
        out_specs=(VMEM,) * 3,
        compiler_params=params,
        name="finish",
    )(own_dq, *kept, *z, *back)


def solution(mesh):
    in_specs = (
        P("pb", "ha", None),
        P("ka", "ha", None),
        P("ka", "ha"),
        P("ka", "ha", None),
        P("pb", "ha", None),
        P("pb", "ha"),
        P("pb", "ha"),
    )
    out_specs = (P(("pb", "ka"), "ha", None), P("ka", "ha", None), P("ka", "ha", None))
    return jax.shard_map(
        per_device, mesh=mesh, in_specs=in_specs, out_specs=out_specs, check_vma=False
    )
```

```python
import functools
import math

import jax
import jax.numpy as jnp
from jax import lax
from jax.experimental import pallas as pl
from jax.experimental.pallas import tpu as pltpu
from jax.sharding import PartitionSpec as P

KEYS_PER_SCALE = 64
LOG2E = math.log2(math.e)
VMEM = pl.BlockSpec(memory_space=pltpu.VMEM)
HBM = pl.BlockSpec(memory_space=pltpu.HBM)
NT = (((1,), (1,)), ((), ()))
SUM_ROWS = 16


def prep_kernel(powers_hbm, codes_hbm, values_hbm, *refs):
    *message_refs, sums_ref, powers_ref, codes_ref, values_ref, sems = refs
    key_count, kv_heads, width = codes_ref.shape
    load_codes = pltpu.make_async_copy(codes_hbm, codes_ref, sems.at[0])
    load_values = pltpu.make_async_copy(values_hbm, values_ref, sems.at[1])
    load_powers = pltpu.make_async_copy(powers_hbm, powers_ref, sems.at[2])
    load_powers.start()
    load_codes.start()
    load_values.start()
    rows = lax.broadcasted_iota(jnp.int32, (key_count, width), 0) // KEYS_PER_SCALE
    factors = []
    load_powers.wait()
    for g in range(kv_heads):
        factor = jnp.zeros((key_count, width), jnp.float32)
        for b in range(key_count // KEYS_PER_SCALE):
            power = jnp.left_shift(1, powers_ref[g, b] + 8).astype(jnp.float32) * 2.0**-8
            factor = jnp.where(rows == b, power, factor)
        factors.append(factor)
    load_codes.wait()
    load_values.wait()
    codes = codes_ref[...].astype(jnp.float32)
    values = values_ref[...].astype(jnp.float32)
    sums = []
    for g in range(kv_heads):
        wide = codes[:, g, :] * factors[g]
        message_refs[g][0:key_count] = wide.astype(jnp.bfloat16)
        message_refs[g][key_count : 2 * key_count] = values[:, g, :].astype(jnp.bfloat16)
        sums.append(jnp.sum(wide, axis=0, keepdims=True))
    line = lax.broadcasted_iota(jnp.int32, (SUM_ROWS, width), 0)
    parts = jnp.zeros((SUM_ROWS, width), jnp.float32)
    whole = jnp.zeros((SUM_ROWS, width), jnp.float32)
    for g in range(kv_heads):
        rest = sums[g]
        whole = jnp.where(line == g, rest, whole)
        for j in range(3):
            piece = rest.astype(jnp.bfloat16).astype(jnp.float32)
            parts = jnp.where(line == 3 * g + j, piece, parts)
            rest = rest - piece
    sums_ref[...] = whole
    for ref in message_refs:
        ref[2 * key_count : 2 * key_count + SUM_ROWS] = parts.astype(jnp.bfloat16)


def gather_kernel(
    row_sets, share, q_hbm, do_hbm, totals_hbm, dots_hbm,
    q_out, do_out, q_ref, do_ref, stats_ref, turned_ref, sems,
):
    ka = lax.axis_index("ka")
    kv_heads = len(row_sets)
    heads, width = q_ref.shape[2:]
    group = heads // kv_heads
    cols = share * group
    loads = []
    for j, src in enumerate((totals_hbm, dots_hbm)):
        load = pltpu.make_async_copy(src, stats_ref.at[pl.ds(j * heads, heads)], sems.at[j])
        load.start()
        loads.append(load)
    needed = sorted({m for sets in row_sets for m in sets})
    for at, m in enumerate(needed):
        for j, (src, dst) in enumerate(((q_hbm, q_ref), (do_hbm, do_ref))):
            load = pltpu.make_async_copy(
                src.at[pl.ds((ka ^ m) * share, share)], dst.at[at], sems.at[2 + 2 * at + j]
            )
            load.start()
            loads.append(load)
    loads[0].wait()
    loads[1].wait()
    stats_ref[pl.ds(2 * heads, width - 2 * heads)] = jnp.zeros(
        (width - 2 * heads, stats_ref.shape[1]), jnp.float32
    )
    rest = stats_ref[...].T
    lane = lax.broadcasted_iota(jnp.int32, rest.shape, 1)
    rest = jnp.where(lane < heads, jnp.clip(rest * LOG2E, -1e38, 1e38), rest)
    terms = jnp.zeros_like(rest)
    for j in range(3):
        piece = rest.astype(jnp.bfloat16).astype(jnp.float32)
        terms = terms + (pltpu.roll(piece, 2 * heads * j, 1) if j else piece)
        rest = rest - piece
    turned_ref[...] = terms
    spot = lax.broadcasted_iota(jnp.int32, (share, group, width), 2) % (2 * heads)
    spot = spot - lax.broadcasted_iota(jnp.int32, (share, group, width), 1)
    for at, m in enumerate(needed):
        rows = turned_ref[pl.ds((ka ^ m) * share, share)]
        rows = jnp.broadcast_to(rows[:, None, :], (share, group, width))
        for j, (src, dst) in enumerate(((q_ref, q_out), (do_ref, do_out))):
            loads[2 + 2 * at + j].wait()
            wide = src[at].astype(jnp.float32)
            for g in range(kv_heads):
                if m in row_sets[g]:
                    to = row_sets[g].index(m)
                    part = wide[:, g * group : (g + 1) * group].reshape(cols, width)
                    dst[g, to, :, 0:width] = part.astype(jnp.bfloat16)
                    extra = jnp.where(spot == j * heads + g * group, rows, 0.0)
                    dst[g, to, :, width:] = extra.reshape(cols, width).astype(jnp.bfloat16)


def rows_kernel(key_devices, share, heads, partners, row_sets, *refs):
    kv_heads = len(partners)
    q_ref, do_ref = refs[:2]
    own_refs, got_refs = refs[2 : 2 + kv_heads], refs[2 + kv_heads : 2 + 2 * kv_heads]
    dq_ref, cross_ref, keep_ref = refs[-3:]
    send_refs = refs[-3 - kv_heads : -3]
    sum_refs = refs[2 + 2 * kv_heads : -3 - kv_heads]
    ka, pb = lax.axis_index("ka"), lax.axis_index("pb")
    cols, width = q_ref.shape[2], q_ref.shape[3] // 2
    key_count = (own_refs[0].shape[0] - SUM_ROWS) // 2
    group = cols // share
    root = width**-0.5
    line = lax.broadcasted_iota(jnp.int32, (2 * key_count, cols), 0)
    step = lax.broadcasted_iota(jnp.int32, (2 * key_count, cols), 1) // group
    lane = lax.broadcasted_iota(jnp.int32, (2 * key_count, width), 1)
    minus = jnp.where(lane < 6 * heads, -1.0, 0.0).astype(jnp.bfloat16)
    parts = own_refs[0][2 * key_count :].astype(jnp.float32)
    for partner in dict(zip(partners, range(kv_heads))).values():
        parts = parts + got_refs[partner][2 * key_count :].astype(jnp.float32)
    whole = jnp.zeros((SUM_ROWS, width), jnp.float32)
    for ref in sum_refs:
        whole = whole + ref[...]
    for g in range(kv_heads):
        own, got = own_refs[g], got_refs[g]
        total = jnp.sum(parts[3 * g : 3 * g + 3], axis=0, keepdims=True) + whole[g : g + 1]
        mean = total / (key_count * key_devices)
        k = jnp.concatenate([own[0:key_count], got[0:key_count]], axis=0).astype(jnp.float32)
        k = (k - mean) * (root * LOG2E)
        turned = k.T.astype(jnp.bfloat16)
        k = jnp.concatenate([k.astype(jnp.bfloat16), minus], axis=1)
        v = jnp.concatenate(
            [own[key_count : 2 * key_count], got[key_count : 2 * key_count]], axis=0
        )
        v = jnp.concatenate([v, minus], axis=1)
        base = jnp.where(line < key_count, ka * key_count, ((ka ^ partners[g]) - 1) * key_count)
        lead = line + base - step
        dk = dv = None
        for at, m in enumerate(row_sets[g]):
            q, do = q_ref[g, at], do_ref[g, at]
            visible = lead <= pb * (share * key_devices) + (ka ^ m) * share
            scores = lax.dot_general(k, q, NT, preferred_element_type=jnp.float32)
            weights = jnp.where(visible, jnp.exp2(scores), 0.0)
            dp = lax.dot_general(v, do, NT, preferred_element_type=jnp.float32)
            ds = (weights * dp).astype(jnp.bfloat16)
            dv_now = jnp.dot(
                weights.astype(jnp.bfloat16), do[:, :width], preferred_element_type=jnp.float32
            )
            dk_now = jnp.dot(ds, q[:, :width], preferred_element_type=jnp.float32)
            dv = dv_now if dv is None else dv + dv_now
            dk = dk_now if dk is None else dk + dk_now
            dq = jnp.dot(turned, ds, preferred_element_type=jnp.float32).T * (1.0 / LOG2E)
            if m == 0:
                dq_ref[g] = dq
            else:
                others = [other for other in row_sets[g] if other]
                send_refs[g][others.index(m)] = dq.astype(jnp.bfloat16)
        for j, grad in ((2 * g, dk * root), (2 * g + 1, dv)):
            keep_ref[j] = grad[:key_count].astype(jnp.bfloat16)
            cross_ref[j] = grad[key_count:].astype(jnp.bfloat16)


def across_kernel(*refs):
    *in_refs, out_a, out_b = refs
    total = in_refs[0][...].astype(jnp.float32)
    for ref in in_refs[1:]:
        total = total + ref[...].astype(jnp.float32)
    half = out_a.shape[0]
    out_a[...] = total[:half].astype(jnp.bfloat16)
    out_b[...] = total[half:].astype(jnp.bfloat16)


def finish_rows_kernel(kv_heads, own_ref, *refs):
    *back_refs, dq_ref = refs
    share, heads, width = dq_ref.shape
    outs = []
    for g in range(kv_heads):
        dq = own_ref[g]
        for ref in back_refs[kv_heads - 1 - g :: kv_heads]:
            dq = dq + ref[...].astype(jnp.float32)
        outs.append(dq.reshape(share, heads // kv_heads, width))
    dq_ref[...] = jnp.concatenate(outs, axis=1).astype(jnp.bfloat16)


def finish_keys_kernel(*refs):
    *keep_refs, z_a, z_b, dk_ref, dv_ref = refs
    total = keep_refs[0][...].astype(jnp.float32)
    for ref in keep_refs[1:]:
        total = total + ref[...].astype(jnp.float32)
    total = total + jnp.concatenate([z_a[...], z_b[...]], axis=0).astype(jnp.float32)
    for j, ref in enumerate((dk_ref, dv_ref)):
        grads = jnp.stack([total[2 * g + j] for g in range(ref.shape[1])], axis=1)
        ref[...] = grads.astype(jnp.bfloat16)


def per_device(queries, key_codes, key_scale_powers, values, grad_out, grad_dot, log_totals):
    query_count, head_count, width = queries.shape
    key_count, kv_heads, _ = key_codes.shape
    group = head_count // kv_heads
    key_devices = lax.axis_size("ka")
    query_devices = lax.axis_size("pb")
    share = query_count // key_devices
    cols = share * group
    params = pltpu.CompilerParams(vmem_limit_bytes=24 * 2**20)
    top = key_devices // 2
    partners = [top if g < kv_heads // 2 else 1 for g in range(kv_heads)]
    row_sets = [[m for m in range(key_devices) if not m & p] for p in partners]
    shape = jax.ShapeDtypeStruct

    def swap(x, by):
        return lax.ppermute(x, "ka", [(i, i ^ by) for i in range(key_devices)])

    def pinned(x):
        return pltpu.with_memory_space_constraint(x, pltpu.HBM)

    *messages, sums = pl.pallas_call(
        prep_kernel,
        out_shape=(shape((2 * key_count + SUM_ROWS, width), jnp.bfloat16),) * kv_heads
        + (shape((SUM_ROWS, width), jnp.float32),),
        in_specs=[HBM, HBM, HBM],
        out_specs=(VMEM,) * (kv_heads + 1),
        scratch_shapes=[
            pltpu.SMEM(key_scale_powers.shape[::-1], jnp.int32),
            pltpu.VMEM(key_codes.shape, key_codes.dtype),
            pltpu.VMEM(values.shape, values.dtype),
            pltpu.SemaphoreType.DMA((3,)),
        ],
        compiler_params=params,
        name="prep",
    )(pinned(key_scale_powers.T), pinned(key_codes), pinned(values))
    got = [swap(message, by) for message, by in zip(messages, partners)]

    others = [swap(sums, by) for by in range(1, key_devices) if by not in partners]
    needed = sorted({m for sets in row_sets for m in sets})
    laid = shape((kv_heads, key_devices // 2, cols, 2 * width), jnp.bfloat16)
    rows_q, rows_do = pl.pallas_call(
        functools.partial(gather_kernel, row_sets, share),
        out_shape=(laid, laid),
        in_specs=[HBM] * 4,
        out_specs=(VMEM,) * 2,
        scratch_shapes=[
            pltpu.VMEM((len(needed), share, head_count, width), queries.dtype),
            pltpu.VMEM((len(needed), share, head_count, width), grad_out.dtype),
            pltpu.VMEM((width, query_count), jnp.float32),
            pltpu.VMEM((query_count, width), jnp.float32),
            pltpu.SemaphoreType.DMA((2 + 2 * len(needed),)),
        ],
        compiler_params=params,
        name="gather",
    )(pinned(queries), pinned(grad_out), pinned(log_totals.T), pinned(grad_dot.T))

    part = shape((2 * kv_heads, key_count, width), jnp.bfloat16)
    sent = shape((key_devices // 2 - 1, cols, width), jnp.bfloat16)
    *sends, own_dq, cross, keep = pl.pallas_call(
        functools.partial(
            rows_kernel, key_devices, share, head_count, partners, row_sets
        ),
        out_shape=(sent,) * kv_heads + (shape((kv_heads, cols, width), jnp.float32), part, part),
        in_specs=[VMEM] * (2 + 2 * kv_heads + len(others)),
        out_specs=(VMEM,) * (kv_heads + 3),
        compiler_params=params,
        name="rows",
    )(rows_q, rows_do, *messages, *got, *others)

    def over_queries(x):
        if query_devices == 2:
            return [x, lax.ppermute(x, "pb", [(0, 1), (1, 0)])]
        return [lax.psum(x.astype(jnp.float32), "pb")]

    crossed = over_queries(cross)
    back = []
    for at in range(key_devices // 2 - 1):
        for g in reversed(range(kv_heads)):
            back.append(swap(sends[g][at], [m for m in row_sets[g] if m][at]))
    kept = over_queries(keep)
    half = shape((kv_heads, key_count, width), jnp.bfloat16)
    z_a, z_b = pl.pallas_call(
        across_kernel,
        out_shape=(half, half),
        in_specs=[VMEM] * len(crossed),
        out_specs=(VMEM, VMEM),
        compiler_params=params,
        cost_estimate=pl.CostEstimate(
            flops=10**10, bytes_accessed=2**20, transcendentals=0
        ),
        name="across",
    )(*crossed)
    z = [swap(z_a, partners[0]), swap(z_b, partners[-1])]
    dq = pl.pallas_call(
        functools.partial(finish_rows_kernel, kv_heads),
        out_shape=shape((share, head_count, width), jnp.bfloat16),
        in_specs=[VMEM] * (1 + len(back)),
        out_specs=VMEM,
        compiler_params=params,
        name="finish_rows",
    )(own_dq, *back)
    dk, dv = pl.pallas_call(
        finish_keys_kernel,
        out_shape=(
            shape(key_codes.shape, jnp.bfloat16),
            shape(values.shape, jnp.bfloat16),
        ),
        in_specs=[VMEM] * (len(kept) + len(z)),
        out_specs=(VMEM, VMEM),
        compiler_params=params,
        name="finish_keys",
    )(*kept, *z)
    return dq, dk, dv


def solution(mesh):
    in_specs = (
        P("pb", "ha", None),
        P("ka", "ha", None),
        P("ka", "ha"),
        P("ka", "ha", None),
        P("pb", "ha", None),
        P("pb", "ha"),
        P("pb", "ha"),
    )
    out_specs = (P(("pb", "ka"), "ha", None), P("ka", "ha", None), P("ka", "ha", None))
    return jax.shard_map(
        per_device, mesh=mesh, in_specs=in_specs, out_specs=out_specs, check_vma=False
    )
```

```python
import functools
import math

import jax
import jax.numpy as jnp
from jax import lax
from jax.experimental import pallas as pl
from jax.experimental.pallas import tpu as pltpu
from jax.sharding import PartitionSpec as P

KEYS_PER_SCALE = 64
LOG2E = math.log2(math.e)
VMEM = pl.BlockSpec(memory_space=pltpu.VMEM)
HBM = pl.BlockSpec(memory_space=pltpu.HBM)
NT = (((1,), (1,)), ((), ()))
SUM_ROWS = 16


def prep_kernel(powers_hbm, codes_hbm, values_hbm, *refs):
    *message_refs, sums_ref, powers_ref, codes_ref, values_ref, sems = refs
    key_count, kv_heads, width = codes_ref.shape
    load_codes = pltpu.make_async_copy(codes_hbm, codes_ref, sems.at[0])
    load_values = pltpu.make_async_copy(values_hbm, values_ref, sems.at[1])
    load_powers = pltpu.make_async_copy(powers_hbm, powers_ref, sems.at[2])
    load_powers.start()
    load_codes.start()
    load_values.start()
    rows = lax.broadcasted_iota(jnp.int32, (key_count, width), 0) // KEYS_PER_SCALE
    factors = []
    load_powers.wait()
    for g in range(kv_heads):
        factor = jnp.zeros((key_count, width), jnp.float32)
        for b in range(key_count // KEYS_PER_SCALE):
            power = jnp.left_shift(1, powers_ref[g, b] + 8).astype(jnp.float32) * 2.0**-8
            factor = jnp.where(rows == b, power, factor)
        factors.append(factor)
    load_codes.wait()
    load_values.wait()
    codes = codes_ref[...].astype(jnp.float32)
    values = values_ref[...].astype(jnp.float32)
    sums = []
    for g in range(kv_heads):
        wide = codes[:, g, :] * factors[g]
        message_refs[g][0:key_count] = wide.astype(jnp.bfloat16)
        message_refs[g][key_count : 2 * key_count] = values[:, g, :].astype(jnp.bfloat16)
        sums.append(jnp.sum(wide, axis=0, keepdims=True))
    line = lax.broadcasted_iota(jnp.int32, (SUM_ROWS, width), 0)
    parts = jnp.zeros((SUM_ROWS, width), jnp.float32)
    whole = jnp.zeros((SUM_ROWS, width), jnp.float32)
    for g in range(kv_heads):
        rest = sums[g]
        whole = jnp.where(line == g, rest, whole)
        for j in range(3):
            piece = rest.astype(jnp.bfloat16).astype(jnp.float32)
            parts = jnp.where(line == 3 * g + j, piece, parts)
            rest = rest - piece
    sums_ref[...] = whole
    for ref in message_refs:
        ref[2 * key_count : 2 * key_count + SUM_ROWS] = parts.astype(jnp.bfloat16)


def gather_kernel(
    row_sets, share, q_hbm, do_hbm, totals_hbm, dots_hbm,
    q_out, do_out, q_ref, do_ref, stats_ref, turned_ref, sems,
):
    ka = lax.axis_index("ka")
    kv_heads = len(row_sets)
    heads, width = q_ref.shape[2:]
    group = heads // kv_heads
    cols = share * group
    loads = []
    for j, src in enumerate((totals_hbm, dots_hbm)):
        load = pltpu.make_async_copy(src, stats_ref.at[pl.ds(j * heads, heads)], sems.at[j])
        load.start()
        loads.append(load)
    needed = sorted({m for sets in row_sets for m in sets})
    for at, m in enumerate(needed):
        for j, (src, dst) in enumerate(((q_hbm, q_ref), (do_hbm, do_ref))):
            load = pltpu.make_async_copy(
                src.at[pl.ds((ka ^ m) * share, share)], dst.at[at], sems.at[2 + 2 * at + j]
            )
            load.start()
            loads.append(load)
    loads[0].wait()
    loads[1].wait()
    stats_ref[pl.ds(2 * heads, width - 2 * heads)] = jnp.zeros(
        (width - 2 * heads, stats_ref.shape[1]), jnp.float32
    )
    rest = stats_ref[...].T
    lane = lax.broadcasted_iota(jnp.int32, rest.shape, 1)
    rest = jnp.where(lane < heads, jnp.clip(rest, -1e36, 1e36) * width**0.5, rest)
    terms = jnp.zeros_like(rest)
    for j in range(3):
        piece = rest.astype(jnp.bfloat16).astype(jnp.float32)
        terms = terms + (pltpu.roll(piece, 2 * heads * j, 1) if j else piece)
        rest = rest - piece
    turned_ref[...] = terms
    spot = lax.broadcasted_iota(jnp.int32, (share, group, width), 2) % (2 * heads)
    spot = spot - lax.broadcasted_iota(jnp.int32, (share, group, width), 1)
    for at, m in enumerate(needed):
        rows = turned_ref[pl.ds((ka ^ m) * share, share)]
        rows = jnp.broadcast_to(rows[:, None, :], (share, group, width))
        for j, (src, dst) in enumerate(((q_ref, q_out), (do_ref, do_out))):
            loads[2 + 2 * at + j].wait()
            wide = src[at].astype(jnp.float32)
            for g in range(kv_heads):
                if m in row_sets[g]:
                    to = row_sets[g].index(m)
                    part = wide[:, g * group : (g + 1) * group].reshape(cols, width)
                    dst[g, to, :, 0:width] = part.astype(jnp.bfloat16)
                    extra = jnp.where(spot == j * heads + g * group, rows, 0.0)
                    dst[g, to, :, width:] = extra.reshape(cols, width).astype(jnp.bfloat16)


def rows_kernel(key_devices, share, heads, partners, row_sets, tasks, first, *refs):
    kv_heads = len(partners)
    busy = [g for g in range(kv_heads) if tasks[g]]
    pieces = 2 if first else 1
    sending = [g for g in busy if any(tasks[g]) for _ in range(pieces)]
    ends = [g for g in range(kv_heads) if partners[g] != partners[0]]
    q_ref, do_ref, *refs = refs
    own_refs, got_refs, refs = refs[:kv_heads], refs[kv_heads : 2 * kv_heads], refs[2 * kv_heads :]
    if first:
        *sum_refs, acc_ref = refs[: -len(sending)]
        send_refs = list(zip(sending, refs[-len(sending) :]))
    else:
        dq_ref, keep_ref = refs[-2 - kv_heads : -kv_heads]
        cross_refs, refs = refs[-kv_heads:], refs[: -2 - kv_heads]
        send_refs = list(zip(sending, refs[-len(sending) :]))
        *sum_refs, acc_ref = refs[: -len(sending)]
    ka, pb = lax.axis_index("ka"), lax.axis_index("pb")
    cols, width = q_ref.shape[2], q_ref.shape[3] // 2
    key_count = (own_refs[0].shape[0] - SUM_ROWS) // 2
    group = cols // share
    root = width**-0.5
    line = lax.broadcasted_iota(jnp.int32, (2 * key_count, cols), 0)
    step = lax.broadcasted_iota(jnp.int32, (2 * key_count, cols), 1) // group
    lane = lax.broadcasted_iota(jnp.int32, (2 * key_count, width), 1)
    minus = jnp.where(lane < 6 * heads, -1.0, 0.0).astype(jnp.bfloat16)
    parts = own_refs[0][2 * key_count :].astype(jnp.float32)
    for partner in dict(zip(partners, range(kv_heads))).values():
        parts = parts + got_refs[partner][2 * key_count :].astype(jnp.float32)
    whole = jnp.zeros((SUM_ROWS, width), jnp.float32)
    for ref in sum_refs:
        whole = whole + ref[...]
    for g in busy:
        own, got = own_refs[g], got_refs[g]
        total = jnp.sum(parts[3 * g : 3 * g + 3], axis=0, keepdims=True) + whole[g : g + 1]
        mean = total / (key_count * key_devices)
        k = jnp.concatenate([own[0:key_count], got[0:key_count]], axis=0).astype(jnp.float32)
        k = (k - mean).astype(jnp.bfloat16)
        turned = k.astype(jnp.float32).T.astype(jnp.bfloat16)
        k = jnp.concatenate([k, minus], axis=1)
        v = jnp.concatenate(
            [own[key_count : 2 * key_count], got[key_count : 2 * key_count]], axis=0
        )
        v = jnp.concatenate([v, minus], axis=1)
        base = jnp.where(line < key_count, ka * key_count, ((ka ^ partners[g]) - 1) * key_count)
        lead = line + base - step
        dk = dv = None
        if not first and g in ends:
            dk, dv = acc_ref[2 * ends.index(g)], acc_ref[2 * ends.index(g) + 1]
        for m in tasks[g]:
            at = row_sets[g].index(m)
            q, do = q_ref[g, at], do_ref[g, at]
            visible = lead <= pb * (share * key_devices) + (ka ^ m) * share
            scores = lax.dot_general(k, q, NT, preferred_element_type=jnp.float32)
            weights = jnp.where(visible, jnp.exp2(scores * (root * LOG2E)), 0.0)
            dp = lax.dot_general(v, do, NT, preferred_element_type=jnp.float32)
            ds = (weights * dp).astype(jnp.bfloat16)
            dv_now = jnp.dot(
                weights.astype(jnp.bfloat16), do[:, :width], preferred_element_type=jnp.float32
            )
            dk_now = jnp.dot(ds, q[:, :width], preferred_element_type=jnp.float32)
            dv = dv_now if dv is None else dv + dv_now
            dk = dk_now if dk is None else dk + dk_now
            dq = jnp.dot(turned, ds, preferred_element_type=jnp.float32).T * root
            if m == 0:
                dq_ref[g] = dq
            else:
                others = [other for other in row_sets[g] if other]
                for j, ref in enumerate(ref for to, ref in send_refs if to == g):
                    piece = dq[j * cols // pieces : (j + 1) * cols // pieces]
                    ref[others.index(m)] = piece.astype(jnp.bfloat16)
        if first:
            acc_ref[2 * ends.index(g)] = dk
            acc_ref[2 * ends.index(g) + 1] = dv
        else:
            for j, grad in enumerate((dk * root, dv)):
                keep_ref[2 * g + j] = grad[:key_count].astype(jnp.bfloat16)
                cross_refs[g][j] = grad[key_count:].astype(jnp.bfloat16)


def across_kernel(after_ref, *refs):
    *in_refs, out_ref = refs
    total = in_refs[0][...].astype(jnp.float32)
    for ref in in_refs[1:]:
        total = total + ref[...].astype(jnp.float32)
    out_ref[...] = total.astype(jnp.bfloat16)


def far_rows_kernel(ends, own_ref, *refs):
    *back_refs, sum_ref = refs
    for j, g in enumerate(ends):
        dq = own_ref[g, : own_ref.shape[1] // 2]
        for ref in back_refs[j :: len(ends)]:
            dq = dq + ref[...].astype(jnp.float32)
        sum_ref[j] = dq


def finish_rows_kernel(ends, late_count, own_ref, far_ref, *refs):
    *back_refs, dq_ref = refs
    late_refs, back_refs = back_refs[:late_count], back_refs[late_count:]
    share, heads, width = dq_ref.shape
    kv_heads = own_ref.shape[0]
    near = [g for g in range(kv_heads) if g not in ends]
    outs = []
    for g in range(kv_heads):
        if g in ends:
            late = own_ref[g, own_ref.shape[1] // 2 :]
            for ref in late_refs[ends.index(g) :: len(ends)]:
                late = late + ref[...].astype(jnp.float32)
            dq = jnp.concatenate([far_ref[ends.index(g)], late], axis=0)
        else:
            dq = own_ref[g]
            for ref in back_refs[near.index(g) :: len(near)]:
                dq = dq + ref[...].astype(jnp.float32)
        outs.append(dq.reshape(share, heads // kv_heads, width))
    dq_ref[...] = jnp.concatenate(outs, axis=1).astype(jnp.bfloat16)


def finish_keys_kernel(*refs):
    *refs, dk_ref, dv_ref = refs
    kv_heads = dk_ref.shape[1]
    keep_refs, z_refs = refs[:-kv_heads], refs[-kv_heads:]
    total = keep_refs[0][...].astype(jnp.float32)
    for ref in keep_refs[1:]:
        total = total + ref[...].astype(jnp.float32)
    total = total + jnp.concatenate([ref[...] for ref in z_refs], axis=0).astype(jnp.float32)
    for j, ref in enumerate((dk_ref, dv_ref)):
        grads = jnp.stack([total[2 * g + j] for g in range(ref.shape[1])], axis=1)
        ref[...] = grads.astype(jnp.bfloat16)


def per_device(queries, key_codes, key_scale_powers, values, grad_out, grad_dot, log_totals):
    query_count, head_count, width = queries.shape
    key_count, kv_heads, _ = key_codes.shape
    group = head_count // kv_heads
    key_devices = lax.axis_size("ka")
    query_devices = lax.axis_size("pb")
    share = query_count // key_devices
    cols = share * group
    params = pltpu.CompilerParams(vmem_limit_bytes=24 * 2**20)
    top = key_devices // 2
    partners = [top if g < kv_heads // 2 else 1 for g in range(kv_heads)]
    row_sets = [[m for m in range(key_devices) if not m & p] for p in partners]
    shape = jax.ShapeDtypeStruct

    def swap(x, by):
        return lax.ppermute(x, "ka", [(i, i ^ by) for i in range(key_devices)])

    def pinned(x):
        return pltpu.with_memory_space_constraint(x, pltpu.HBM)

    *messages, sums = pl.pallas_call(
        prep_kernel,
        out_shape=(shape((2 * key_count + SUM_ROWS, width), jnp.bfloat16),) * kv_heads
        + (shape((SUM_ROWS, width), jnp.float32),),
        in_specs=[HBM, HBM, HBM],
        out_specs=(VMEM,) * (kv_heads + 1),
        scratch_shapes=[
            pltpu.SMEM(key_scale_powers.shape[::-1], jnp.int32),
            pltpu.VMEM(key_codes.shape, key_codes.dtype),
            pltpu.VMEM(values.shape, values.dtype),
            pltpu.SemaphoreType.DMA((3,)),
        ],
        compiler_params=params,
        name="prep",
    )(pinned(key_scale_powers.T), pinned(key_codes), pinned(values))
    got = [swap(message, by) for message, by in zip(messages, partners)]

    others = [swap(sums, by) for by in range(1, key_devices) if by not in partners]
    needed = sorted({m for sets in row_sets for m in sets})
    laid = shape((kv_heads, key_devices // 2, cols, 2 * width), jnp.bfloat16)
    rows_q, rows_do = pl.pallas_call(
        functools.partial(gather_kernel, row_sets, share),
        out_shape=(laid, laid),
        in_specs=[HBM] * 4,
        out_specs=(VMEM,) * 2,
        scratch_shapes=[
            pltpu.VMEM((len(needed), share, head_count, width), queries.dtype),
            pltpu.VMEM((len(needed), share, head_count, width), grad_out.dtype),
            pltpu.VMEM((width, query_count), jnp.float32),
            pltpu.VMEM((query_count, width), jnp.float32),
            pltpu.SemaphoreType.DMA((2 + 2 * len(needed),)),
        ],
        compiler_params=params,
        name="gather",
    )(pinned(queries), pinned(grad_out), pinned(log_totals.T), pinned(grad_dot.T))

    part = shape((2 * kv_heads, key_count, width), jnp.bfloat16)
    sent = shape((key_devices // 2 - 1, cols, width), jnp.bfloat16)
    half_sent = shape((key_devices // 2 - 1, cols // 2, width), jnp.bfloat16)
    near = [g for g in range(kv_heads) if partners[g] == partners[0]]
    ends = [g for g in range(kv_heads) if partners[g] != partners[0]]
    inputs = (rows_q, rows_do, *messages, *got, *others)

    def rows(tasks, first, *extra, out_shape):
        return pl.pallas_call(
            functools.partial(
                rows_kernel, key_devices, share, head_count, partners, row_sets, tasks, first
            ),
            out_shape=out_shape,
            in_specs=[VMEM] * (len(inputs) + len(extra)),
            out_specs=(VMEM,) * len(out_shape),
            compiler_params=params,
            name="far_rows" if first else "near_rows",
        )(*inputs, *extra)

    acc, *far_sends = rows(
        [[m for m in row_sets[g] if m] if g in ends else [] for g in range(kv_heads)],
        True,
        out_shape=(shape((2 * len(ends), 2 * key_count, width), jnp.float32),)
        + (half_sent,) * (2 * len(ends)),
    )
    one = shape((2, key_count, width), jnp.bfloat16)
    results = rows(
        [[0] if g in ends else row_sets[g] for g in range(kv_heads)],
        False,
        acc,
        out_shape=(sent,) * len(near)
        + (shape((kv_heads, cols, width), jnp.float32), part)
        + (one,) * kv_heads,
    )
    near_sends, crosses = results[: len(near)], results[len(near) + 2 :]
    own_dq, keep = results[len(near) : len(near) + 2]

    def send_back(sends, heads):
        return [
            swap(send[at], [m for m in row_sets[g] if m][at])
            for at in range(key_devices // 2 - 1)
            for send, g in zip(sends, heads)
        ]

    far_back = send_back(far_sends[0::2], ends)
    far_late = send_back(far_sends[1::2], ends)
    near_back = send_back(near_sends, near)

    def over_queries(x):
        if query_devices == 2:
            return [x, lax.ppermute(x, "pb", [(0, 1), (1, 0)])]
        return [lax.psum(x.astype(jnp.float32), "pb")]

    far_dq = pl.pallas_call(
        functools.partial(far_rows_kernel, ends),
        out_shape=shape((len(ends), cols // 2, width), jnp.float32),
        in_specs=[VMEM] * (1 + len(far_back)),
        out_specs=VMEM,
        compiler_params=params,
        cost_estimate=pl.CostEstimate(flops=10**10, bytes_accessed=2**20, transcendentals=0),
        name="far_dq",
    )(own_dq, *far_back)
    z = []
    for cross, partner in zip(crosses, partners):
        crossed = over_queries(cross)
        summed = pl.pallas_call(
            across_kernel,
            out_shape=one,
            in_specs=[pl.BlockSpec(memory_space=pl.ANY)] + [VMEM] * len(crossed),
            out_specs=VMEM,
            compiler_params=params,
            name="across",
        )(far_dq, *crossed)
        z.append(swap(summed, partner))
    kept = over_queries(keep)
    dq = pl.pallas_call(
        functools.partial(finish_rows_kernel, ends, len(far_late)),
        out_shape=shape((share, head_count, width), jnp.bfloat16),
        in_specs=[VMEM] * (2 + len(far_late) + len(near_back)),
        out_specs=VMEM,
        compiler_params=params,
        name="finish_rows",
    )(own_dq, far_dq, *far_late, *near_back)
    dk, dv = pl.pallas_call(
        finish_keys_kernel,
        out_shape=(
            shape(key_codes.shape, jnp.bfloat16),
            shape(values.shape, jnp.bfloat16),
        ),
        in_specs=[VMEM] * (len(kept) + len(z)),
        out_specs=(VMEM, VMEM),
        compiler_params=params,
        name="finish_keys",
    )(*kept, *z)
    return dq, dk, dv


def solution(mesh):
    in_specs = (
        P("pb", "ha", None),
        P("ka", "ha", None),
        P("ka", "ha"),
        P("ka", "ha", None),
        P("pb", "ha", None),
        P("pb", "ha"),
        P("pb", "ha"),
    )
    out_specs = (P(("pb", "ka"), "ha", None), P("ka", "ha", None), P("ka", "ha", None))
    return jax.shard_map(
        per_device, mesh=mesh, in_specs=in_specs, out_specs=out_specs, check_vma=False
    )
```

```python
import functools
import math

import jax
import jax.numpy as jnp
from jax import lax
from jax.experimental import pallas as pl
from jax.experimental.pallas import tpu as pltpu
from jax.sharding import PartitionSpec as P

KEYS_PER_SCALE = 64
LOG2E = math.log2(math.e)
VMEM = pl.BlockSpec(memory_space=pltpu.VMEM)
HBM = pl.BlockSpec(memory_space=pltpu.HBM)
NT = (((1,), (1,)), ((), ()))
SUM_ROWS = 16


def prep_kernel(powers_hbm, codes_hbm, values_hbm, *refs):
    *message_refs, sums_ref, powers_ref, codes_ref, values_ref, sems = refs
    key_count, kv_heads, width = codes_ref.shape
    load_codes = pltpu.make_async_copy(codes_hbm, codes_ref, sems.at[0])
    load_values = pltpu.make_async_copy(values_hbm, values_ref, sems.at[1])
    load_powers = pltpu.make_async_copy(powers_hbm, powers_ref, sems.at[2])
    load_powers.start()
    load_codes.start()
    load_values.start()
    rows = lax.broadcasted_iota(jnp.int32, (key_count, width), 0) // KEYS_PER_SCALE
    factors = []
    load_powers.wait()
    for g in range(kv_heads):
        factor = jnp.zeros((key_count, width), jnp.float32)
        for b in range(key_count // KEYS_PER_SCALE):
            power = jnp.left_shift(1, powers_ref[g, b] + 8).astype(jnp.float32) * 2.0**-8
            factor = jnp.where(rows == b, power, factor)
        factors.append(factor)
    load_codes.wait()
    load_values.wait()
    codes = codes_ref[...].astype(jnp.float32)
    values = values_ref[...].astype(jnp.float32)
    sums = []
    for g in range(kv_heads):
        wide = codes[:, g, :] * factors[g]
        message_refs[g][0:key_count] = wide.astype(jnp.bfloat16)
        message_refs[g][key_count : 2 * key_count] = values[:, g, :].astype(jnp.bfloat16)
        sums.append(jnp.sum(wide, axis=0, keepdims=True))
    line = lax.broadcasted_iota(jnp.int32, (SUM_ROWS, width), 0)
    parts = jnp.zeros((SUM_ROWS, width), jnp.float32)
    whole = jnp.zeros((SUM_ROWS, width), jnp.float32)
    for g in range(kv_heads):
        rest = sums[g]
        whole = jnp.where(line == g, rest, whole)
        for j in range(3):
            piece = rest.astype(jnp.bfloat16).astype(jnp.float32)
            parts = jnp.where(line == 3 * g + j, piece, parts)
            rest = rest - piece
    sums_ref[...] = whole
    for ref in message_refs:
        ref[2 * key_count : 2 * key_count + SUM_ROWS] = parts.astype(jnp.bfloat16)


def gather_kernel(
    row_sets, share, q_hbm, do_hbm, totals_hbm, dots_hbm,
    q_out, do_out, q_ref, do_ref, stats_ref, turned_ref, sems,
):
    ka = lax.axis_index("ka")
    kv_heads = len(row_sets)
    heads, width = q_ref.shape[2:]
    group = heads // kv_heads
    cols = share * group
    loads = []
    for j, src in enumerate((totals_hbm, dots_hbm)):
        load = pltpu.make_async_copy(src, stats_ref.at[pl.ds(j * heads, heads)], sems.at[j])
        load.start()
        loads.append(load)
    needed = sorted({m for sets in row_sets for m in sets})
    for at, m in enumerate(needed):
        for j, (src, dst) in enumerate(((q_hbm, q_ref), (do_hbm, do_ref))):
            load = pltpu.make_async_copy(
                src.at[pl.ds((ka ^ m) * share, share)], dst.at[at], sems.at[2 + 2 * at + j]
            )
            load.start()
            loads.append(load)
    loads[0].wait()
    loads[1].wait()
    stats_ref[pl.ds(2 * heads, width - 2 * heads)] = jnp.zeros(
        (width - 2 * heads, stats_ref.shape[1]), jnp.float32
    )
    rest = stats_ref[...].T
    lane = lax.broadcasted_iota(jnp.int32, rest.shape, 1)
    rest = jnp.where(lane < heads, jnp.clip(rest, -1e36, 1e36) * width**0.5, rest)
    terms = jnp.zeros_like(rest)
    for j in range(3):
        piece = rest.astype(jnp.bfloat16).astype(jnp.float32)
        terms = terms + (pltpu.roll(piece, 2 * heads * j, 1) if j else piece)
        rest = rest - piece
    turned_ref[...] = terms
    spot = lax.broadcasted_iota(jnp.int32, (share, group, width), 2) % (2 * heads)
    spot = spot - lax.broadcasted_iota(jnp.int32, (share, group, width), 1)
    for at, m in enumerate(needed):
        rows = turned_ref[pl.ds((ka ^ m) * share, share)]
        rows = jnp.broadcast_to(rows[:, None, :], (share, group, width))
        for j, (src, dst) in enumerate(((q_ref, q_out), (do_ref, do_out))):
            loads[2 + 2 * at + j].wait()
            wide = src[at].astype(jnp.float32)
            for g in range(kv_heads):
                if m in row_sets[g]:
                    to = row_sets[g].index(m)
                    part = wide[:, g * group : (g + 1) * group].reshape(cols, width)
                    dst[g, to, :, 0:width] = part.astype(jnp.bfloat16)
                    extra = jnp.where(spot == j * heads + g * group, rows, 0.0)
                    dst[g, to, :, width:] = extra.reshape(cols, width).astype(jnp.bfloat16)


def rows_kernel(key_devices, share, heads, partners, row_sets, tasks, first, *refs):
    kv_heads = len(partners)
    busy = [g for g in range(kv_heads) if tasks[g]]
    pieces = 1
    sending = [g for g in busy if any(tasks[g]) for _ in range(pieces)]
    ends = [g for g in range(kv_heads) if partners[g] != partners[0]]
    q_ref, do_ref, *refs = refs
    own_refs, got_refs, refs = refs[:kv_heads], refs[kv_heads : 2 * kv_heads], refs[2 * kv_heads :]
    dq_ref, keep_ref = refs[-2 - kv_heads : -kv_heads]
    cross_refs, refs = refs[-kv_heads:], refs[: -2 - kv_heads]
    send_refs = list(zip(sending, refs[-len(sending) :]))
    sum_refs = refs[: -len(sending)]
    ka, pb = lax.axis_index("ka"), lax.axis_index("pb")
    cols, width = q_ref.shape[2], q_ref.shape[3] // 2
    key_count = (own_refs[0].shape[0] - SUM_ROWS) // 2
    group = cols // share
    root = width**-0.5
    line = lax.broadcasted_iota(jnp.int32, (2 * key_count, cols), 0)
    step = lax.broadcasted_iota(jnp.int32, (2 * key_count, cols), 1) // group
    lane = lax.broadcasted_iota(jnp.int32, (2 * key_count, width), 1)
    minus = jnp.where(lane < 6 * heads, -1.0, 0.0).astype(jnp.bfloat16)
    parts = own_refs[0][2 * key_count :].astype(jnp.float32)
    for partner in dict(zip(partners, range(kv_heads))).values():
        parts = parts + got_refs[partner][2 * key_count :].astype(jnp.float32)
    whole = jnp.zeros((SUM_ROWS, width), jnp.float32)
    for ref in sum_refs:
        whole = whole + ref[...]
    for g in busy:
        own, got = own_refs[g], got_refs[g]
        total = jnp.sum(parts[3 * g : 3 * g + 3], axis=0, keepdims=True) + whole[g : g + 1]
        mean = total / (key_count * key_devices)
        k = jnp.concatenate([own[0:key_count], got[0:key_count]], axis=0).astype(jnp.float32)
        k = (k - mean).astype(jnp.bfloat16)
        turned = k.astype(jnp.float32).T.astype(jnp.bfloat16)
        k = jnp.concatenate([k, minus], axis=1)
        v = jnp.concatenate(
            [own[key_count : 2 * key_count], got[key_count : 2 * key_count]], axis=0
        )
        v = jnp.concatenate([v, minus], axis=1)
        base = jnp.where(line < key_count, ka * key_count, ((ka ^ partners[g]) - 1) * key_count)
        lead = line + base - step
        dk = dv = None
        for m in tasks[g]:
            at = row_sets[g].index(m)
            q, do = q_ref[g, at], do_ref[g, at]
            visible = lead <= pb * (share * key_devices) + (ka ^ m) * share
            scores = lax.dot_general(k, q, NT, preferred_element_type=jnp.float32)
            weights = jnp.where(visible, jnp.exp2(scores * (root * LOG2E)), 0.0)
            dp = lax.dot_general(v, do, NT, preferred_element_type=jnp.float32)
            ds = (weights * dp).astype(jnp.bfloat16)
            dv_now = jnp.dot(
                weights.astype(jnp.bfloat16), do[:, :width], preferred_element_type=jnp.float32
            )
            dk_now = jnp.dot(ds, q[:, :width], preferred_element_type=jnp.float32)
            dv = dv_now if dv is None else dv + dv_now
            dk = dk_now if dk is None else dk + dk_now
            dq = jnp.dot(turned, ds, preferred_element_type=jnp.float32).T * root
            if m == 0:
                dq_ref[g] = dq
            else:
                others = [other for other in row_sets[g] if other]
                for j, ref in enumerate(ref for to, ref in send_refs if to == g):
                    piece = dq[j * cols // pieces : (j + 1) * cols // pieces]
                    ref[others.index(m)] = piece.astype(jnp.bfloat16)
        for j, grad in enumerate((dk * root, dv)):
            keep_ref[2 * g + j] = grad[:key_count]
            cross_refs[g][j] = grad[key_count:].astype(jnp.bfloat16)


def join_kernel(keep_ref, *refs):
    *got_refs, out_ref = refs
    for g, ref in enumerate(got_refs):
        total = keep_ref[2 * g : 2 * g + 2] + ref[...].astype(jnp.float32)
        out_ref[2 * g : 2 * g + 2] = total.astype(jnp.bfloat16)


def finish_kernel(kept_count, own_ref, *refs):
    *refs, dq_ref, dk_ref, dv_ref = refs
    kept_refs, back_refs = refs[:kept_count], refs[kept_count:]
    share, heads, width = dq_ref.shape
    kv_heads = own_ref.shape[0]
    outs = []
    for g in range(kv_heads):
        dq = own_ref[g]
        for ref in back_refs[kv_heads - 1 - g :: kv_heads]:
            dq = dq + ref[...].astype(jnp.float32)
        outs.append(dq.reshape(share, heads // kv_heads, width))
    dq_ref[...] = jnp.concatenate(outs, axis=1).astype(jnp.bfloat16)
    total = kept_refs[0][...].astype(jnp.float32)
    for ref in kept_refs[1:]:
        total = total + ref[...].astype(jnp.float32)
    for j, ref in enumerate((dk_ref, dv_ref)):
        grads = jnp.stack([total[2 * g + j] for g in range(kv_heads)], axis=1)
        ref[...] = grads.astype(jnp.bfloat16)


def per_device(queries, key_codes, key_scale_powers, values, grad_out, grad_dot, log_totals):
    query_count, head_count, width = queries.shape
    key_count, kv_heads, _ = key_codes.shape
    group = head_count // kv_heads
    key_devices = lax.axis_size("ka")
    query_devices = lax.axis_size("pb")
    share = query_count // key_devices
    cols = share * group
    params = pltpu.CompilerParams(vmem_limit_bytes=24 * 2**20)
    top = key_devices // 2
    partners = [1 if g < kv_heads // 2 else top for g in range(kv_heads)]
    row_sets = [[m for m in range(key_devices) if not m & p] for p in partners]
    shape = jax.ShapeDtypeStruct

    def swap(x, by):
        return lax.ppermute(x, "ka", [(i, i ^ by) for i in range(key_devices)])

    def pinned(x):
        return pltpu.with_memory_space_constraint(x, pltpu.HBM)

    *messages, sums = pl.pallas_call(
        prep_kernel,
        out_shape=(shape((2 * key_count + SUM_ROWS, width), jnp.bfloat16),) * kv_heads
        + (shape((SUM_ROWS, width), jnp.float32),),
        in_specs=[HBM, HBM, HBM],
        out_specs=(VMEM,) * (kv_heads + 1),
        scratch_shapes=[
            pltpu.SMEM(key_scale_powers.shape[::-1], jnp.int32),
            pltpu.VMEM(key_codes.shape, key_codes.dtype),
            pltpu.VMEM(values.shape, values.dtype),
            pltpu.SemaphoreType.DMA((3,)),
        ],
        compiler_params=params,
        name="prep",
    )(pinned(key_scale_powers.T), pinned(key_codes), pinned(values))
    got = [swap(message, by) for message, by in zip(messages, partners)]

    others = [swap(sums, by) for by in range(1, key_devices) if by not in partners]
    needed = sorted({m for sets in row_sets for m in sets})
    laid = shape((kv_heads, key_devices // 2, cols, 2 * width), jnp.bfloat16)
    rows_q, rows_do = pl.pallas_call(
        functools.partial(gather_kernel, row_sets, share),
        out_shape=(laid, laid),
        in_specs=[HBM] * 4,
        out_specs=(VMEM,) * 2,
        scratch_shapes=[
            pltpu.VMEM((len(needed), share, head_count, width), queries.dtype),
            pltpu.VMEM((len(needed), share, head_count, width), grad_out.dtype),
            pltpu.VMEM((width, query_count), jnp.float32),
            pltpu.VMEM((query_count, width), jnp.float32),
            pltpu.SemaphoreType.DMA((2 + 2 * len(needed),)),
        ],
        compiler_params=params,
        name="gather",
    )(pinned(queries), pinned(grad_out), pinned(log_totals.T), pinned(grad_dot.T))

    part = shape((2 * kv_heads, key_count, width), jnp.bfloat16)
    whole_part = shape((2 * kv_heads, key_count, width), jnp.float32)
    one = shape((2, key_count, width), jnp.bfloat16)
    sent = shape((key_devices // 2 - 1, cols, width), jnp.bfloat16)
    near = [g for g in range(kv_heads) if partners[g] == partners[0]]
    ends = [g for g in range(kv_heads) if partners[g] != partners[0]]
    inputs = (rows_q, rows_do, *messages, *got, *others)

    def rows(tasks, first, *extra, out_shape):
        return pl.pallas_call(
            functools.partial(
                rows_kernel, key_devices, share, head_count, partners, row_sets, tasks, first
            ),
            out_shape=out_shape,
            in_specs=[VMEM] * (len(inputs) + len(extra)),
            out_specs=(VMEM,) * len(out_shape),
            compiler_params=params,
            name="far_rows" if first else "near_rows",
        )(*inputs, *extra)

    results = rows(
        row_sets,
        False,
        out_shape=(sent,) * kv_heads
        + (shape((kv_heads, cols, width), jnp.float32), whole_part)
        + (one,) * kv_heads,
    )
    sends, crosses = results[:kv_heads], results[kv_heads + 2 :]
    own_dq, keep = results[kv_heads : kv_heads + 2]

    def send_back(sends, heads):
        return [
            swap(send[at], [m for m in row_sets[g] if m][at])
            for at in range(key_devices // 2 - 1)
            for send, g in zip(sends, heads)
        ]

    back = send_back(sends[::-1], list(range(kv_heads))[::-1])

    def over_queries(x):
        if query_devices == 2:
            return [x, lax.ppermute(x, "pb", [(0, 1), (1, 0)])]
        return [lax.psum(x.astype(jnp.float32), "pb")]

    mine = pl.pallas_call(
        join_kernel,
        out_shape=part,
        in_specs=[VMEM] * (1 + kv_heads),
        out_specs=VMEM,
        compiler_params=params,
        cost_estimate=pl.CostEstimate(flops=10**10, bytes_accessed=2**20, transcendentals=0),
        name="join",
    )(keep, *[swap(cross, by) for cross, by in zip(crosses, partners)])
    kept = over_queries(mine)
    arrived = (own_dq, *kept, *back)
    return pl.pallas_call(
        functools.partial(finish_kernel, len(kept)),
        out_shape=(
            shape((share, head_count, width), jnp.bfloat16),
            shape(key_codes.shape, jnp.bfloat16),
            shape(values.shape, jnp.bfloat16),
        ),
        in_specs=[VMEM] * len(arrived),
        out_specs=(VMEM,) * 3,
        compiler_params=params,
        name="finish",
    )(*arrived)


def solution(mesh):
    in_specs = (
        P("pb", "ha", None),
        P("ka", "ha", None),
        P("ka", "ha"),
        P("ka", "ha", None),
        P("pb", "ha", None),
        P("pb", "ha"),
        P("pb", "ha"),
    )
    out_specs = (P(("pb", "ka"), "ha", None), P("ka", "ha", None), P("ka", "ha", None))
    return jax.shard_map(
        per_device, mesh=mesh, in_specs=in_specs, out_specs=out_specs, check_vma=False
    )
```

```python
import functools
import math

import jax
import jax.numpy as jnp
from jax import lax
from jax.experimental import pallas as pl
from jax.experimental.pallas import tpu as pltpu
from jax.sharding import PartitionSpec as P

KEYS_PER_SCALE = 64
LOG2E = math.log2(math.e)
VMEM = pl.BlockSpec(memory_space=pltpu.VMEM)
HBM = pl.BlockSpec(memory_space=pltpu.HBM)
NT = (((1,), (1,)), ((), ()))
SUM_ROWS = 16


def prep_kernel(powers_hbm, codes_hbm, values_hbm, *refs):
    *message_refs, sums_ref, powers_ref, codes_ref, values_ref, sems = refs
    key_count, kv_heads, width = codes_ref.shape
    load_codes = pltpu.make_async_copy(codes_hbm, codes_ref, sems.at[0])
    load_values = pltpu.make_async_copy(values_hbm, values_ref, sems.at[1])
    load_powers = pltpu.make_async_copy(powers_hbm, powers_ref, sems.at[2])
    load_powers.start()
    load_codes.start()
    load_values.start()
    rows = lax.broadcasted_iota(jnp.int32, (key_count, width), 0) // KEYS_PER_SCALE
    factors = []
    load_powers.wait()
    for g in range(kv_heads):
        factor = jnp.zeros((key_count, width), jnp.float32)
        for b in range(key_count // KEYS_PER_SCALE):
            power = jnp.left_shift(1, powers_ref[g, b] + 8).astype(jnp.float32) * 2.0**-8
            factor = jnp.where(rows == b, power, factor)
        factors.append(factor)
    load_codes.wait()
    load_values.wait()
    codes = codes_ref[...].astype(jnp.float32)
    values = values_ref[...].astype(jnp.float32)
    sums = []
    for g in range(kv_heads):
        wide = codes[:, g, :] * factors[g]
        message_refs[g][0:key_count] = wide.astype(jnp.bfloat16)
        message_refs[g][key_count : 2 * key_count] = values[:, g, :].astype(jnp.bfloat16)
        sums.append(jnp.sum(wide, axis=0, keepdims=True))
    line = lax.broadcasted_iota(jnp.int32, (SUM_ROWS, width), 0)
    parts = jnp.zeros((SUM_ROWS, width), jnp.float32)
    whole = jnp.zeros((SUM_ROWS, width), jnp.float32)
    for g in range(kv_heads):
        rest = sums[g]
        whole = jnp.where(line == g, rest, whole)
        for j in range(3):
            piece = rest.astype(jnp.bfloat16).astype(jnp.float32)
            parts = jnp.where(line == 3 * g + j, piece, parts)
            rest = rest - piece
    sums_ref[...] = whole
    for ref in message_refs:
        ref[2 * key_count : 2 * key_count + SUM_ROWS] = parts.astype(jnp.bfloat16)


def gather_kernel(
    row_sets, share, q_hbm, do_hbm, totals_hbm, dots_hbm,
    q_out, do_out, q_ref, do_ref, stats_ref, turned_ref, sems,
):
    ka = lax.axis_index("ka")
    kv_heads = len(row_sets)
    heads, width = q_ref.shape[2:]
    group = heads // kv_heads
    cols = share * group
    loads = []
    for j, src in enumerate((totals_hbm, dots_hbm)):
        load = pltpu.make_async_copy(src, stats_ref.at[pl.ds(j * heads, heads)], sems.at[j])
        load.start()
        loads.append(load)
    needed = sorted({m for sets in row_sets for m in sets})
    for at, m in enumerate(needed):
        for j, (src, dst) in enumerate(((q_hbm, q_ref), (do_hbm, do_ref))):
            load = pltpu.make_async_copy(
                src.at[pl.ds((ka ^ m) * share, share)], dst.at[at], sems.at[2 + 2 * at + j]
            )
            load.start()
            loads.append(load)
    loads[0].wait()
    loads[1].wait()
    stats_ref[pl.ds(2 * heads, width - 2 * heads)] = jnp.zeros(
        (width - 2 * heads, stats_ref.shape[1]), jnp.float32
    )
    rest = stats_ref[...].T
    lane = lax.broadcasted_iota(jnp.int32, rest.shape, 1)
    rest = jnp.where(lane < heads, jnp.clip(rest, -1e36, 1e36) * width**0.5, rest)
    terms = jnp.zeros_like(rest)
    for j in range(3):
        piece = rest.astype(jnp.bfloat16).astype(jnp.float32)
        terms = terms + (pltpu.roll(piece, 2 * heads * j, 1) if j else piece)
        rest = rest - piece
    turned_ref[...] = terms
    spot = lax.broadcasted_iota(jnp.int32, (share, group, width), 2) % (2 * heads)
    spot = spot - lax.broadcasted_iota(jnp.int32, (share, group, width), 1)
    for at, m in enumerate(needed):
        rows = turned_ref[pl.ds((ka ^ m) * share, share)]
        rows = jnp.broadcast_to(rows[:, None, :], (share, group, width))
        for j, (src, dst) in enumerate(((q_ref, q_out), (do_ref, do_out))):
            loads[2 + 2 * at + j].wait()
            wide = src[at].astype(jnp.float32)
            for g in range(kv_heads):
                if m in row_sets[g]:
                    to = row_sets[g].index(m)
                    part = wide[:, g * group : (g + 1) * group].reshape(cols, width)
                    dst[g, to, :, 0:width] = part.astype(jnp.bfloat16)
                    extra = jnp.where(spot == j * heads + g * group, rows, 0.0)
                    dst[g, to, :, width:] = extra.reshape(cols, width).astype(jnp.bfloat16)


def rows_kernel(key_devices, share, heads, partners, row_sets, first, *refs):
    kv_heads = len(partners)
    q_ref, do_ref, *refs = refs
    own_refs, got_refs, refs = refs[:kv_heads], refs[kv_heads : 2 * kv_heads], refs[2 * kv_heads :]
    if first:
        part_ref, *cross_refs = refs[-1 - kv_heads :]
        sum_refs = refs[: -1 - kv_heads]
    else:
        *sum_refs, part_ref = refs[: -2 - kv_heads]
        *send_refs, dq_ref, keep_ref = refs[-2 - kv_heads :]
    ka, pb = lax.axis_index("ka"), lax.axis_index("pb")
    cols, width = q_ref.shape[2], q_ref.shape[3] // 2
    key_count = (own_refs[0].shape[0] - SUM_ROWS) // 2
    group = cols // share
    root = width**-0.5
    lead = lax.broadcasted_iota(jnp.int32, (key_count, cols), 0)
    lead = lead - lax.broadcasted_iota(jnp.int32, (key_count, cols), 1) // group
    lane = lax.broadcasted_iota(jnp.int32, (key_count, width), 1)
    minus = jnp.where(lane < 6 * heads, -1.0, 0.0).astype(jnp.bfloat16)
    parts = own_refs[0][2 * key_count :].astype(jnp.float32)
    for partner in dict(zip(partners, range(kv_heads))).values():
        parts = parts + got_refs[partner][2 * key_count :].astype(jnp.float32)
    whole = jnp.zeros((SUM_ROWS, width), jnp.float32)
    for ref in sum_refs:
        whole = whole + ref[...]
    for g in range(kv_heads):
        message = got_refs[g] if first else own_refs[g]
        total = jnp.sum(parts[3 * g : 3 * g + 3], axis=0, keepdims=True) + whole[g : g + 1]
        mean = total / (key_count * key_devices)
        k = (message[0:key_count].astype(jnp.float32) - mean).astype(jnp.bfloat16)
        turned = k.astype(jnp.float32).T.astype(jnp.bfloat16)
        k = jnp.concatenate([k, minus], axis=1)
        v = jnp.concatenate([message[key_count : 2 * key_count], minus], axis=1)
        base = (ka ^ partners[g] if first else ka) * key_count
        dk = dv = None
        for at, m in enumerate(row_sets[g]):
            q, do = q_ref[g, at], do_ref[g, at]
            visible = lead <= pb * (share * key_devices) + (ka ^ m) * share - base
            scores = lax.dot_general(k, q, NT, preferred_element_type=jnp.float32)
            weights = jnp.where(visible, jnp.exp2(scores * (root * LOG2E)), 0.0)
            dp = lax.dot_general(v, do, NT, preferred_element_type=jnp.float32)
            ds = (weights * dp).astype(jnp.bfloat16)
            dv_now = jnp.dot(
                weights.astype(jnp.bfloat16), do[:, :width], preferred_element_type=jnp.float32
            )
            dk_now = jnp.dot(ds, q[:, :width], preferred_element_type=jnp.float32)
            dv = dv_now if dv is None else dv + dv_now
            dk = dk_now if dk is None else dk + dk_now
            dq = jnp.dot(turned, ds, preferred_element_type=jnp.float32)
            if first:
                part_ref[g, at] = dq
                continue
            dq = (dq + part_ref[g, at]).T * root
            if m == 0:
                dq_ref[g] = dq
            else:
                others = [other for other in row_sets[g] if other]
                send_refs[g][others.index(m)] = dq.astype(jnp.bfloat16)
        for j, grad in enumerate((dk * root, dv)):
            if first:
                cross_refs[g][j] = grad.astype(jnp.bfloat16)
            else:
                keep_ref[2 * g + j] = grad


def join_kernel(keep_ref, *refs):
    *got_refs, out_ref = refs
    for g, ref in enumerate(got_refs):
        total = keep_ref[2 * g : 2 * g + 2] + ref[...].astype(jnp.float32)
        out_ref[2 * g : 2 * g + 2] = total.astype(jnp.bfloat16)


def finish_kernel(kept_count, own_ref, *refs):
    *refs, dq_ref, dk_ref, dv_ref = refs
    kept_refs, back_refs = refs[:kept_count], refs[kept_count:]
    share, heads, width = dq_ref.shape
    kv_heads = own_ref.shape[0]
    outs = []
    for g in range(kv_heads):
        dq = own_ref[g]
        for ref in back_refs[g::kv_heads]:
            dq = dq + ref[...].astype(jnp.float32)
        outs.append(dq.reshape(share, heads // kv_heads, width))
    dq_ref[...] = jnp.concatenate(outs, axis=1).astype(jnp.bfloat16)
    total = kept_refs[0][...].astype(jnp.float32)
    for ref in kept_refs[1:]:
        total = total + ref[...].astype(jnp.float32)
    for j, ref in enumerate((dk_ref, dv_ref)):
        grads = jnp.stack([total[2 * g + j] for g in range(kv_heads)], axis=1)
        ref[...] = grads.astype(jnp.bfloat16)


def per_device(queries, key_codes, key_scale_powers, values, grad_out, grad_dot, log_totals):
    query_count, head_count, width = queries.shape
    key_count, kv_heads, _ = key_codes.shape
    group = head_count // kv_heads
    key_devices = lax.axis_size("ka")
    query_devices = lax.axis_size("pb")
    share = query_count // key_devices
    cols = share * group
    params = pltpu.CompilerParams(vmem_limit_bytes=24 * 2**20)
    top = key_devices // 2
    partners = [1 if g < kv_heads // 2 else top for g in range(kv_heads)]
    row_sets = [[m for m in range(key_devices) if not m & p] for p in partners]
    shape = jax.ShapeDtypeStruct

    def swap(x, by):
        return lax.ppermute(x, "ka", [(i, i ^ by) for i in range(key_devices)])

    def pinned(x):
        return pltpu.with_memory_space_constraint(x, pltpu.HBM)

    *messages, sums = pl.pallas_call(
        prep_kernel,
        out_shape=(shape((2 * key_count + SUM_ROWS, width), jnp.bfloat16),) * kv_heads
        + (shape((SUM_ROWS, width), jnp.float32),),
        in_specs=[HBM, HBM, HBM],
        out_specs=(VMEM,) * (kv_heads + 1),
        scratch_shapes=[
            pltpu.SMEM(key_scale_powers.shape[::-1], jnp.int32),
            pltpu.VMEM(key_codes.shape, key_codes.dtype),
            pltpu.VMEM(values.shape, values.dtype),
            pltpu.SemaphoreType.DMA((3,)),
        ],
        compiler_params=params,
        name="prep",
    )(pinned(key_scale_powers.T), pinned(key_codes), pinned(values))
    got = [swap(message, by) for message, by in zip(messages, partners)]

    others = [swap(sums, by) for by in range(1, key_devices) if by not in partners]
    needed = sorted({m for sets in row_sets for m in sets})
    laid = shape((kv_heads, key_devices // 2, cols, 2 * width), jnp.bfloat16)
    rows_q, rows_do = pl.pallas_call(
        functools.partial(gather_kernel, row_sets, share),
        out_shape=(laid, laid),
        in_specs=[HBM] * 4,
        out_specs=(VMEM,) * 2,
        scratch_shapes=[
            pltpu.VMEM((len(needed), share, head_count, width), queries.dtype),
            pltpu.VMEM((len(needed), share, head_count, width), grad_out.dtype),
            pltpu.VMEM((width, query_count), jnp.float32),
            pltpu.VMEM((query_count, width), jnp.float32),
            pltpu.SemaphoreType.DMA((2 + 2 * len(needed),)),
        ],
        compiler_params=params,
        name="gather",
    )(pinned(queries), pinned(grad_out), pinned(log_totals.T), pinned(grad_dot.T))

    part = shape((2 * kv_heads, key_count, width), jnp.bfloat16)
    whole_part = shape((2 * kv_heads, key_count, width), jnp.float32)
    one = shape((2, key_count, width), jnp.bfloat16)
    sent = shape((key_devices // 2 - 1, cols, width), jnp.bfloat16)
    near = [g for g in range(kv_heads) if partners[g] == partners[0]]
    ends = [g for g in range(kv_heads) if partners[g] != partners[0]]
    inputs = (rows_q, rows_do, *messages, *got, *others)

    def rows(first, *extra, out_shape):
        return pl.pallas_call(
            functools.partial(
                rows_kernel, key_devices, share, head_count, partners, row_sets, first
            ),
            out_shape=out_shape,
            in_specs=[VMEM] * (len(inputs) + len(extra)),
            out_specs=(VMEM,) * len(out_shape),
            compiler_params=params,
            name="partner_keys" if first else "own_keys",
        )(*inputs, *extra)

    handed, *crosses = rows(
        True,
        out_shape=(shape((kv_heads, key_devices // 2, width, cols), jnp.float32),)
        + (one,) * kv_heads,
    )
    *sends, own_dq, keep = rows(
        False,
        handed,
        out_shape=(sent,) * kv_heads + (shape((kv_heads, cols, width), jnp.float32), whole_part),
    )

    def send_back(sends, heads):
        return [
            swap(send[at], [m for m in row_sets[g] if m][at])
            for at in range(key_devices // 2 - 1)
            for send, g in zip(sends, heads)
        ]

    back = send_back(sends, list(range(kv_heads)))

    def over_queries(x):
        if query_devices == 2:
            return [x, lax.ppermute(x, "pb", [(0, 1), (1, 0)])]
        return [lax.psum(x.astype(jnp.float32), "pb")]

    mine = pl.pallas_call(
        join_kernel,
        out_shape=part,
        in_specs=[VMEM] * (1 + kv_heads),
        out_specs=VMEM,
        compiler_params=params,
        cost_estimate=pl.CostEstimate(flops=10**10, bytes_accessed=2**20, transcendentals=0),
        name="join",
    )(keep, *[swap(cross, by) for cross, by in zip(crosses, partners)])
    kept = over_queries(mine)
    arrived = (own_dq, *kept, *back)
    return pl.pallas_call(
        functools.partial(finish_kernel, len(kept)),
        out_shape=(
            shape((share, head_count, width), jnp.bfloat16),
            shape(key_codes.shape, jnp.bfloat16),
            shape(values.shape, jnp.bfloat16),
        ),
        in_specs=[VMEM] * len(arrived),
        out_specs=(VMEM,) * 3,
        compiler_params=params,
        name="finish",
    )(*arrived)


def solution(mesh):
    in_specs = (
        P("pb", "ha", None),
        P("ka", "ha", None),
        P("ka", "ha"),
        P("ka", "ha", None),
        P("pb", "ha", None),
        P("pb", "ha"),
        P("pb", "ha"),
    )
    out_specs = (P(("pb", "ka"), "ha", None), P("ka", "ha", None), P("ka", "ha", None))
    return jax.shard_map(
        per_device, mesh=mesh, in_specs=in_specs, out_specs=out_specs, check_vma=False
    )
```

```python
import functools
import math

import jax
import jax.numpy as jnp
from jax import lax
from jax.experimental import pallas as pl
from jax.experimental.pallas import tpu as pltpu
from jax.sharding import PartitionSpec as P

KEYS_PER_SCALE = 64
LOG2E = math.log2(math.e)
VMEM = pl.BlockSpec(memory_space=pltpu.VMEM)
HBM = pl.BlockSpec(memory_space=pltpu.HBM)
NT = (((1,), (1,)), ((), ()))
SUM_ROWS = 16


def prep_kernel(powers_hbm, codes_hbm, values_hbm, *refs):
    *message_refs, sums_ref, powers_ref, codes_ref, values_ref, sems = refs
    key_count, kv_heads, width = codes_ref.shape
    load_codes = pltpu.make_async_copy(codes_hbm, codes_ref, sems.at[0])
    load_values = pltpu.make_async_copy(values_hbm, values_ref, sems.at[1])
    load_powers = pltpu.make_async_copy(powers_hbm, powers_ref, sems.at[2])
    load_powers.start()
    load_codes.start()
    load_values.start()
    rows = lax.broadcasted_iota(jnp.int32, (key_count, width), 0) // KEYS_PER_SCALE
    factors = []
    load_powers.wait()
    for g in range(kv_heads):
        factor = jnp.zeros((key_count, width), jnp.float32)
        for b in range(key_count // KEYS_PER_SCALE):
            power = jnp.left_shift(1, powers_ref[g, b] + 8).astype(jnp.float32) * 2.0**-8
            factor = jnp.where(rows == b, power, factor)
        factors.append(factor)
    load_codes.wait()
    load_values.wait()
    codes = codes_ref[...].astype(jnp.float32)
    values = values_ref[...].astype(jnp.float32)
    sums = []
    for g in range(kv_heads):
        wide = codes[:, g, :] * factors[g]
        message_refs[g][0:key_count] = wide.astype(jnp.bfloat16)
        message_refs[g][key_count : 2 * key_count] = values[:, g, :].astype(jnp.bfloat16)
        sums.append(jnp.sum(wide, axis=0, keepdims=True))
    line = lax.broadcasted_iota(jnp.int32, (SUM_ROWS, width), 0)
    parts = jnp.zeros((SUM_ROWS, width), jnp.float32)
    whole = jnp.zeros((SUM_ROWS, width), jnp.float32)
    for g in range(kv_heads):
        rest = sums[g]
        whole = jnp.where(line == g, rest, whole)
        for j in range(3):
            piece = rest.astype(jnp.bfloat16).astype(jnp.float32)
            parts = jnp.where(line == 3 * g + j, piece, parts)
            rest = rest - piece
    sums_ref[...] = whole
    for ref in message_refs:
        ref[2 * key_count : 2 * key_count + SUM_ROWS] = parts.astype(jnp.bfloat16)


def gather_kernel(
    row_sets, share, q_hbm, do_hbm, totals_hbm, dots_hbm,
    q_out, do_out, q_ref, do_ref, stats_ref, turned_ref, sems,
):
    ka = lax.axis_index("ka")
    kv_heads = len(row_sets)
    heads, width = q_ref.shape[2:]
    group = heads // kv_heads
    cols = share * group
    loads = []
    for j, src in enumerate((totals_hbm, dots_hbm)):
        load = pltpu.make_async_copy(src, stats_ref.at[pl.ds(j * heads, heads)], sems.at[j])
        load.start()
        loads.append(load)
    needed = sorted({m for sets in row_sets for m in sets})
    for at, m in enumerate(needed):
        for j, (src, dst) in enumerate(((q_hbm, q_ref), (do_hbm, do_ref))):
            load = pltpu.make_async_copy(
                src.at[pl.ds((ka ^ m) * share, share)], dst.at[at], sems.at[2 + 2 * at + j]
            )
            load.start()
            loads.append(load)
    loads[0].wait()
    loads[1].wait()
    stats_ref[pl.ds(2 * heads, width - 2 * heads)] = jnp.zeros(
        (width - 2 * heads, stats_ref.shape[1]), jnp.float32
    )
    rest = stats_ref[...].T
    lane = lax.broadcasted_iota(jnp.int32, rest.shape, 1)
    rest = jnp.where(lane < heads, jnp.clip(rest, -1e36, 1e36) * width**0.5, rest)
    terms = jnp.zeros_like(rest)
    for j in range(3):
        piece = rest.astype(jnp.bfloat16).astype(jnp.float32)
        terms = terms + (pltpu.roll(piece, 2 * heads * j, 1) if j else piece)
        rest = rest - piece
    turned_ref[...] = terms
    spot = lax.broadcasted_iota(jnp.int32, (share, group, width), 2) % (2 * heads)
    spot = spot - lax.broadcasted_iota(jnp.int32, (share, group, width), 1)
    for at, m in enumerate(needed):
        rows = turned_ref[pl.ds((ka ^ m) * share, share)]
        rows = jnp.broadcast_to(rows[:, None, :], (share, group, width))
        for j, (src, dst) in enumerate(((q_ref, q_out), (do_ref, do_out))):
            loads[2 + 2 * at + j].wait()
            wide = src[at].astype(jnp.float32)
            for g in range(kv_heads):
                if m in row_sets[g]:
                    to = row_sets[g].index(m)
                    part = wide[:, g * group : (g + 1) * group].reshape(cols, width)
                    dst[g, to, :, 0:width] = part.astype(jnp.bfloat16)
                    extra = jnp.where(spot == j * heads + g * group, rows, 0.0)
                    dst[g, to, :, width:] = extra.reshape(cols, width).astype(jnp.bfloat16)


def rows_kernel(key_devices, share, heads, partners, row_sets, first, *refs):
    kv_heads = len(partners)
    q_ref, do_ref, *refs = refs
    own_refs, got_refs, refs = refs[:kv_heads], refs[kv_heads : 2 * kv_heads], refs[2 * kv_heads :]
    if first:
        part_ref, *cross_refs = refs[-1 - kv_heads :]
        sum_refs = refs[: -1 - kv_heads]
    else:
        *sum_refs, part_ref = refs[: -2 - kv_heads]
        *send_refs, dq_ref, keep_ref = refs[-2 - kv_heads :]
    ka, pb = lax.axis_index("ka"), lax.axis_index("pb")
    cols, width = q_ref.shape[2], q_ref.shape[3] // 2
    key_count = (own_refs[0].shape[0] - SUM_ROWS) // 2
    group = cols // share
    root = width**-0.5
    lead = lax.broadcasted_iota(jnp.int32, (key_count, cols), 0)
    lead = lead - lax.broadcasted_iota(jnp.int32, (key_count, cols), 1) // group
    lane = lax.broadcasted_iota(jnp.int32, (key_count, width), 1)
    minus = jnp.where(lane < 6 * heads, -1.0, 0.0).astype(jnp.bfloat16)
    parts = own_refs[0][2 * key_count :].astype(jnp.float32)
    for partner in dict(zip(partners, range(kv_heads))).values():
        parts = parts + got_refs[partner][2 * key_count :].astype(jnp.float32)
    whole = jnp.zeros((SUM_ROWS, width), jnp.float32)
    for ref in sum_refs:
        whole = whole + ref[...]
    for g in range(kv_heads):
        message = got_refs[g] if first else own_refs[g]
        total = jnp.sum(parts[3 * g : 3 * g + 3], axis=0, keepdims=True) + whole[g : g + 1]
        mean = total / (key_count * key_devices)
        k = (message[0:key_count].astype(jnp.float32) - mean).astype(jnp.bfloat16)
        turned = k.astype(jnp.float32).T.astype(jnp.bfloat16)
        k = jnp.concatenate([k, minus], axis=1)
        v = jnp.concatenate([message[key_count : 2 * key_count], minus], axis=1)
        base = (ka ^ partners[g] if first else ka) * key_count
        dk = dv = None
        for at, m in enumerate(row_sets[g]):
            q, do = q_ref[g, at], do_ref[g, at]
            visible = lead <= pb * (share * key_devices) + (ka ^ m) * share - base
            scores = lax.dot_general(k, q, NT, preferred_element_type=jnp.float32)
            weights = jnp.where(visible, jnp.exp2(scores * (root * LOG2E)), 0.0)
            dp = lax.dot_general(v, do, NT, preferred_element_type=jnp.float32)
            ds = (weights * dp).astype(jnp.bfloat16)
            dv_now = jnp.dot(
                weights.astype(jnp.bfloat16), do[:, :width], preferred_element_type=jnp.float32
            )
            dk_now = jnp.dot(ds, q[:, :width], preferred_element_type=jnp.float32)
            dv = dv_now if dv is None else dv + dv_now
            dk = dk_now if dk is None else dk + dk_now
            dq = jnp.dot(turned, ds, preferred_element_type=jnp.float32)
            if first:
                part_ref[g, at] = dq
                continue
            dq = (dq + part_ref[g, at]).T * root
            if m == 0:
                dq_ref[g] = dq
            else:
                others = [other for other in row_sets[g] if other]
                send_refs[g][others.index(m)] = dq.astype(jnp.bfloat16)
        for j, grad in enumerate((dk * root, dv)):
            if first:
                cross_refs[g][j] = grad.astype(jnp.bfloat16)
            else:
                keep_ref[2 * g + j] = grad


def join_kernel(g, keep_ref, got_ref, out_ref):
    total = keep_ref[2 * g : 2 * g + 2] + got_ref[...].astype(jnp.float32)
    out_ref[...] = total.astype(jnp.bfloat16)


def finish_kernel(kept_count, own_ref, *refs):
    *refs, dq_ref, dk_ref, dv_ref = refs
    kept_refs, back_refs = refs[:kept_count], refs[kept_count:]
    share, heads, width = dq_ref.shape
    kv_heads = own_ref.shape[0]
    outs = []
    for g in range(kv_heads):
        dq = own_ref[g]
        for ref in back_refs[g::kv_heads]:
            dq = dq + ref[...].astype(jnp.float32)
        outs.append(dq.reshape(share, heads // kv_heads, width))
    dq_ref[...] = jnp.concatenate(outs, axis=1).astype(jnp.bfloat16)
    each = kept_count // kv_heads
    totals = []
    for g in range(kv_heads):
        total = kept_refs[g * each][...].astype(jnp.float32)
        for ref in kept_refs[g * each + 1 : (g + 1) * each]:
            total = total + ref[...].astype(jnp.float32)
        totals.append(total)
    for j, ref in enumerate((dk_ref, dv_ref)):
        grads = jnp.stack([total[j] for total in totals], axis=1)
        ref[...] = grads.astype(jnp.bfloat16)


def per_device(queries, key_codes, key_scale_powers, values, grad_out, grad_dot, log_totals):
    query_count, head_count, width = queries.shape
    key_count, kv_heads, _ = key_codes.shape
    group = head_count // kv_heads
    key_devices = lax.axis_size("ka")
    query_devices = lax.axis_size("pb")
    share = query_count // key_devices
    cols = share * group
    params = pltpu.CompilerParams(vmem_limit_bytes=24 * 2**20)
    top = key_devices // 2
    partners = [1 if g < kv_heads // 2 else top for g in range(kv_heads)]
    row_sets = [[m for m in range(key_devices) if not m & p] for p in partners]
    shape = jax.ShapeDtypeStruct

    def swap(x, by):
        return lax.ppermute(x, "ka", [(i, i ^ by) for i in range(key_devices)])

    def pinned(x):
        return pltpu.with_memory_space_constraint(x, pltpu.HBM)

    *messages, sums = pl.pallas_call(
        prep_kernel,
        out_shape=(shape((2 * key_count + SUM_ROWS, width), jnp.bfloat16),) * kv_heads
        + (shape((SUM_ROWS, width), jnp.float32),),
        in_specs=[HBM, HBM, HBM],
        out_specs=(VMEM,) * (kv_heads + 1),
        scratch_shapes=[
            pltpu.SMEM(key_scale_powers.shape[::-1], jnp.int32),
            pltpu.VMEM(key_codes.shape, key_codes.dtype),
            pltpu.VMEM(values.shape, values.dtype),
            pltpu.SemaphoreType.DMA((3,)),
        ],
        compiler_params=params,
        name="prep",
    )(pinned(key_scale_powers.T), pinned(key_codes), pinned(values))
    got = [swap(message, by) for message, by in zip(messages, partners)]

    others = [swap(sums, by) for by in range(1, key_devices) if by not in partners]
    needed = sorted({m for sets in row_sets for m in sets})
    laid = shape((kv_heads, key_devices // 2, cols, 2 * width), jnp.bfloat16)
    rows_q, rows_do = pl.pallas_call(
        functools.partial(gather_kernel, row_sets, share),
        out_shape=(laid, laid),
        in_specs=[HBM] * 4,
        out_specs=(VMEM,) * 2,
        scratch_shapes=[
            pltpu.VMEM((len(needed), share, head_count, width), queries.dtype),
            pltpu.VMEM((len(needed), share, head_count, width), grad_out.dtype),
            pltpu.VMEM((width, query_count), jnp.float32),
            pltpu.VMEM((query_count, width), jnp.float32),
            pltpu.SemaphoreType.DMA((2 + 2 * len(needed),)),
        ],
        compiler_params=params,
        name="gather",
    )(pinned(queries), pinned(grad_out), pinned(log_totals.T), pinned(grad_dot.T))

    whole_part = shape((2 * kv_heads, key_count, width), jnp.float32)
    one = shape((2, key_count, width), jnp.bfloat16)
    sent = shape((key_devices // 2 - 1, cols, width), jnp.bfloat16)
    near = [g for g in range(kv_heads) if partners[g] == partners[0]]
    ends = [g for g in range(kv_heads) if partners[g] != partners[0]]
    inputs = (rows_q, rows_do, *messages, *got, *others)

    def rows(first, *extra, out_shape):
        return pl.pallas_call(
            functools.partial(
                rows_kernel, key_devices, share, head_count, partners, row_sets, first
            ),
            out_shape=out_shape,
            in_specs=[VMEM] * (len(inputs) + len(extra)),
            out_specs=(VMEM,) * len(out_shape),
            compiler_params=params,
            name="partner_keys" if first else "own_keys",
        )(*inputs, *extra)

    handed, *crosses = rows(
        True,
        out_shape=(shape((kv_heads, key_devices // 2, width, cols), jnp.float32),)
        + (one,) * kv_heads,
    )
    *sends, own_dq, keep = rows(
        False,
        handed,
        out_shape=(sent,) * kv_heads + (shape((kv_heads, cols, width), jnp.float32), whole_part),
    )

    def send_back(sends, heads):
        return [
            swap(send[at], [m for m in row_sets[g] if m][at])
            for at in range(key_devices // 2 - 1)
            for send, g in zip(sends, heads)
        ]

    back = send_back(sends, list(range(kv_heads)))

    def over_queries(x):
        if query_devices == 2:
            return [x, lax.ppermute(x, "pb", [(0, 1), (1, 0)])]
        return [lax.psum(x.astype(jnp.float32), "pb")]

    kept = []
    for g, (cross, partner) in enumerate(zip(crosses, partners)):
        mine = pl.pallas_call(
            functools.partial(join_kernel, g),
            out_shape=one,
            in_specs=[VMEM] * 2,
            out_specs=VMEM,
            compiler_params=params,
            cost_estimate=pl.CostEstimate(
                flops=10**10, bytes_accessed=2**20, transcendentals=0
            ),
            name="join",
        )(keep, swap(cross, partner))
        kept += over_queries(mine)
    arrived = (own_dq, *kept, *back)
    return pl.pallas_call(
        functools.partial(finish_kernel, len(kept)),
        out_shape=(
            shape((share, head_count, width), jnp.bfloat16),
            shape(key_codes.shape, jnp.bfloat16),
            shape(values.shape, jnp.bfloat16),
        ),
        in_specs=[VMEM] * len(arrived),
        out_specs=(VMEM,) * 3,
        compiler_params=params,
        name="finish",
    )(*arrived)


def solution(mesh):
    in_specs = (
        P("pb", "ha", None),
        P("ka", "ha", None),
        P("ka", "ha"),
        P("ka", "ha", None),
        P("pb", "ha", None),
        P("pb", "ha"),
        P("pb", "ha"),
    )
    out_specs = (P(("pb", "ka"), "ha", None), P("ka", "ha", None), P("ka", "ha", None))
    return jax.shard_map(
        per_device, mesh=mesh, in_specs=in_specs, out_specs=out_specs, check_vma=False
    )
```
